512 devices in a mesh: dp: 16 (over y_hi, x, core), expert: 32 (over y_lo, z).
Axes of the slice: x: 4, y: 4 (y_hi: 2, y_lo: 2; y = y_hi * 2 + y_lo), z: 16, core: 2. Of those that a mesh axis runs over, the one named last changes fastest.
Arguments:
- tokens: bfloat16 [8192, 5120], P(('dp', 'expert')), may hold values from -6 to 6
- out_grad: bfloat16 [8192, 5120], P(('dp', 'expert')), may hold values from -6 to 6
- expert_index: int32 [8192, 2], P(('dp', 'expert')), may hold values from 0 to 3, as said below
- slot: int32 [8192, 2], P(('dp', 'expert')), may hold values from -1 to 9, as said below
- gate: bfloat16 [8192, 2], P(('dp', 'expert')), may hold values from 0.19921875 to 1
- w_gate: bfloat16 [32, 5120, 128], P('expert'), may hold values from -0.078125 to 0.078125
- w_up: bfloat16 [32, 5120, 128], P('expert'), may hold values from -0.078125 to 0.078125
- w_down: bfloat16 [32, 5120, 128], P('expert'), may hold values from -0.1875 to 0.1875
Outputs:
- input_grad: bfloat16 [8192, 5120], P(('dp', 'expert'))
- grad_gate: bfloat16 [32, 5120, 128], P('expert', 'dp')
- grad_up: bfloat16 [32, 5120, 128], P('expert', 'dp')
- grad_down: bfloat16 [32, 5120, 128], P('expert', 'dp')
The draws below stay inside these ranges and needn't reach their ends.
Inputs may be any that keep to these rules, and one draw needn't show every extreme that they name: `expert_index`: each row names 2 different experts. `slot`: within the 16 tokens of one device, the routes to one expert, taken in order of token and then route, get slots 0, 1, 2 and so on; routes past the capacity get -1. In every draw some expert is full on every device.
All inputs are finite; a program needn't handle non-finite values.
Results may differ from the reference program's by a relative error of at most 0.017.
Values may be sent and summed in bfloat16 or wider, within the bound.
No kernel may reach another device: no remote copies, remote signals or barrier semaphores. Data moves between devices by JAX's collectives and lax.ppermute only.
A program may use at most 64 MiB of HBM per device.

```python
import jax
import jax.numpy as jnp
from jax import lax

MODEL_WIDTH = 5120
H_DEV = 128
WINDOW_EXPERTS = 4
TOP = 2
TOK_DEV = 16
SLOT_CAPACITY = 10
SPLIT = 8
HIDDEN_SIZE = 1024
SLICES = 32
TOKENS = 8192
N_DP = 16
N_EXPERT = 32


def route_tables(key):
    key_fav, key_score, key_perm = jax.random.split(key, 3)
    blocks = N_DP * N_EXPERT
    favored = jax.random.randint(key_fav, (N_DP,), 0, WINDOW_EXPERTS)
    favored_tok = jnp.repeat(favored, N_EXPERT * TOK_DEV)
    scores = jax.random.randint(key_score, (TOKENS, WINDOW_EXPERTS), 0, 4096) * WINDOW_EXPERTS
    scores = scores + jnp.arange(WINDOW_EXPERTS, dtype=jnp.int32)[None, :]
    perm_keys = jax.random.split(key_perm, blocks)
    order = jax.vmap(lambda k: jax.random.permutation(k, TOK_DEV))(perm_keys).reshape(TOKENS)
    boosted = order < min(TOK_DEV, SLOT_CAPACITY + 2)
    match = jnp.arange(WINDOW_EXPERTS, dtype=jnp.int32)[None, :] == favored_tok[:, None]
    scores = scores + jnp.where(boosted[:, None] & match, 2 ** 24, 0)
    _, chosen = lax.top_k(scores, TOP)
    chosen = chosen.astype(jnp.int32)
    onehot = (chosen[:, :, None] == jnp.arange(WINDOW_EXPERTS, dtype=jnp.int32)).astype(jnp.int32)
    onehot = onehot.reshape(blocks, TOK_DEV * TOP, WINDOW_EXPERTS)
    before = jnp.cumsum(onehot, axis=1) - onehot
    position = jnp.sum(before * onehot, axis=2).reshape(TOKENS, TOP)
    position = jnp.where(position < SLOT_CAPACITY, position, -1).astype(jnp.int32)
    return (chosen, position)


def draw_expert_index(key, part):
    chosen, position = route_tables(key)
    return chosen


def draw_slot(key, part):
    chosen, position = route_tables(key)
    return position


def levels(key, shape, pieces, low, top_value):
    gain = 1.0
    for dim, shards_of in pieces:
        draws = jax.random.uniform(jax.random.fold_in(jax.random.fold_in(key, 6), dim), (shards_of,), jnp.float32, low / len(pieces), top_value / len(pieces))
        gain = gain * jnp.repeat(jnp.exp(draws), shape[dim] // shards_of).reshape((-1,) + (1,) * (len(shape) - 1 - dim))
    return gain


def centred(key, shape, scale, most, shards=(), kind=jnp.bfloat16):
    level = levels(key, shape, shards, -0.22, 0.18) if shards else 1.0
    entries = jax.random.normal(key, shape, jnp.float32) * scale * level
    return jnp.minimum(jnp.maximum(entries, -most), most).astype(kind)


def setup_inputs(seed: int = 0) -> dict:
    arg_keys = jax.random.split(jax.random.key(seed), 9)
    tokens = centred(arg_keys[0], (TOKENS, MODEL_WIDTH), 1.0, 6.0, ((0, 512),))
    out_grad = centred(arg_keys[1], (TOKENS, MODEL_WIDTH), 1.0, 6.0, ((0, 512),))
    expert_index = draw_expert_index(jax.random.fold_in(arg_keys[8], 71), 0)
    slot = draw_slot(jax.random.fold_in(arg_keys[8], 71), 0)
    gate = jnp.clip(0.19921875 + 0.80078125 * jax.random.uniform(arg_keys[4], (TOKENS, TOP), jnp.float32) ** levels(arg_keys[4], (TOKENS, TOP), ((0, 512),), -0.2, 0.2), 0.19921875, 1.0).astype(jnp.bfloat16)
    w_gate = centred(arg_keys[5], (SLICES, MODEL_WIDTH, H_DEV), MODEL_WIDTH ** -0.5, 0.078125, ((0, 32),))
    w_up = centred(arg_keys[6], (SLICES, MODEL_WIDTH, H_DEV), MODEL_WIDTH ** -0.5, 0.078125, ((0, 32),))
    w_down = centred(arg_keys[7], (SLICES, MODEL_WIDTH, H_DEV), HIDDEN_SIZE ** -0.5, 0.1875, ((0, 32),))
    return {"tokens": tokens, "out_grad": out_grad, "expert_index": expert_index, "slot": slot, "gate": gate, "w_gate": w_gate, "w_up": w_up, "w_down": w_down}


def expert_tables(idx_src, pos_src):
    flat = jnp.where(pos_src >= 0, idx_src * SLOT_CAPACITY + pos_src, WINDOW_EXPERTS * SLOT_CAPACITY).reshape(-1)
    return flat


def group_step(carry, inputs):
    x_g, output_gradient_gathered, idx_g, pos_g, gate_g, gate_weight_complete, up_weight_complete, down_weight_complete = inputs
    tok_ids = jnp.repeat(jnp.arange(TOK_DEV, dtype=jnp.int32), TOP)

    def tables(idx_src, pos_src, gate_src):
        flat = expert_tables(idx_src, pos_src)
        slot_tok = jnp.zeros((WINDOW_EXPERTS * SLOT_CAPACITY + 1,), jnp.int32).at[flat].set(tok_ids)[:-1]
        capacity_gate_weight = jnp.zeros((WINDOW_EXPERTS * SLOT_CAPACITY + 1,), jnp.float32).at[flat].set(gate_src.reshape(-1).astype(jnp.float32))[:-1]
        live = jnp.zeros((WINDOW_EXPERTS * SLOT_CAPACITY + 1,), jnp.float32).at[flat].set(1.0)[:-1]
        return flat, slot_tok, capacity_gate_weight, live

    flats, slot_tok, capacity_gate_weight, live = jax.vmap(tables)(idx_g, pos_g, gate_g)
    token_rows = slot_tok + (jnp.arange(N_EXPERT, dtype=jnp.int32) * TOK_DEV)[:, None]
    input_holder = (x_g[token_rows].astype(jnp.float32) * live[:, :, None]).astype(jnp.bfloat16)
    gradient_holder = (output_gradient_gathered[token_rows].astype(jnp.float32) * capacity_gate_weight[:, :, None]).astype(jnp.bfloat16)
    input_holder = input_holder.reshape(N_EXPERT, WINDOW_EXPERTS, SLOT_CAPACITY, MODEL_WIDTH).transpose(1, 0, 2, 3).reshape(WINDOW_EXPERTS, N_EXPERT * SLOT_CAPACITY, MODEL_WIDTH)
    gradient_holder = gradient_holder.reshape(N_EXPERT, WINDOW_EXPERTS, SLOT_CAPACITY, MODEL_WIDTH).transpose(1, 0, 2, 3).reshape(WINDOW_EXPERTS, N_EXPERT * SLOT_CAPACITY, MODEL_WIDTH)

    def expert_results(items):
        xe, ge, wg, wu, wd = items
        act_a = jnp.dot(xe, wg, preferred_element_type=jnp.float32)
        act_b = jnp.dot(xe, wu, preferred_element_type=jnp.float32)
        grad_h = jnp.dot(ge, wd, preferred_element_type=jnp.float32)
        sig = jax.nn.sigmoid(act_a)
        silu = act_a * sig
        hidden = (silu * act_b).astype(jnp.bfloat16)
        grad_a = (grad_h * act_b * sig * (1.0 + act_a * (1.0 - sig))).astype(jnp.bfloat16)
        grad_b = (grad_h * silu).astype(jnp.bfloat16)
        dwg = jnp.dot(xe.T, grad_a, preferred_element_type=jnp.float32).astype(jnp.bfloat16).astype(jnp.float32)
        dwu = jnp.dot(xe.T, grad_b, preferred_element_type=jnp.float32).astype(jnp.bfloat16).astype(jnp.float32)
        dwd = jnp.dot(ge.T, hidden, preferred_element_type=jnp.float32).astype(jnp.bfloat16).astype(jnp.float32)
        nrow = xe.shape[0]
        da_s = grad_a.astype(jnp.float32).reshape(nrow, SPLIT, H_DEV)
        db_s = grad_b.astype(jnp.float32).reshape(nrow, SPLIT, H_DEV)
        wg_s = wg.astype(jnp.float32).reshape(MODEL_WIDTH, SPLIT, H_DEV)
        wu_s = wu.astype(jnp.float32).reshape(MODEL_WIDTH, SPLIT, H_DEV)
        part = jnp.einsum('rsh,dsh->srd', da_s, wg_s) + jnp.einsum('rsh,dsh->srd', db_s, wu_s)
        part = part.astype(jnp.bfloat16).astype(jnp.float32)
        return jnp.stack([dwg, dwu, dwd]), jnp.sum(part, axis=0)

    weight_gradient_list, input_gradient_total = lax.map(expert_results, (input_holder, gradient_holder, gate_weight_complete, up_weight_complete, down_weight_complete))
    input_gradient_total = input_gradient_total.reshape(WINDOW_EXPERTS, N_EXPERT, SLOT_CAPACITY, MODEL_WIDTH).transpose(1, 0, 2, 3).reshape(N_EXPERT, WINDOW_EXPERTS * SLOT_CAPACITY, MODEL_WIDTH)
    input_gradient_total = jnp.concatenate([input_gradient_total, jnp.zeros((N_EXPERT, 1, MODEL_WIDTH), jnp.float32)], axis=1)
    picked = jax.vmap(lambda table, flat: table[flat])(input_gradient_total, flats)
    dx_g = jnp.sum(picked.reshape(N_EXPERT, TOK_DEV, TOP, MODEL_WIDTH), axis=2).reshape(N_EXPERT * TOK_DEV, MODEL_WIDTH)
    return carry + weight_gradient_list.transpose(1, 0, 2, 3), dx_g.astype(jnp.bfloat16)


def reference(tokens, out_grad, expert_index, slot, gate, w_gate, w_up, w_down):
    def full(weight):
        return weight.reshape(WINDOW_EXPERTS, SPLIT, MODEL_WIDTH, H_DEV).transpose(0, 2, 1, 3).reshape(WINDOW_EXPERTS, MODEL_WIDTH, SPLIT * H_DEV)

    gate_weight_complete, up_weight_complete, down_weight_complete = full(w_gate), full(w_up), full(w_down)
    per_group = (
        tokens.reshape(N_DP, N_EXPERT * TOK_DEV, MODEL_WIDTH),
        out_grad.reshape(N_DP, N_EXPERT * TOK_DEV, MODEL_WIDTH),
        expert_index.reshape(N_DP, N_EXPERT, TOK_DEV, TOP),
        slot.reshape(N_DP, N_EXPERT, TOK_DEV, TOP),
        gate.reshape(N_DP, N_EXPERT, TOK_DEV, TOP),
    )

    def step(carry, items):
        return group_step(carry, items + (gate_weight_complete, up_weight_complete, down_weight_complete))

    init = jnp.zeros((3, WINDOW_EXPERTS, MODEL_WIDTH, SPLIT * H_DEV), jnp.float32)
    total, dx = lax.scan(step, init, per_group)
    total = total.astype(jnp.bfloat16).reshape(3, WINDOW_EXPERTS, MODEL_WIDTH, SPLIT, H_DEV).transpose(0, 1, 3, 2, 4)
    total = total.reshape(3, WINDOW_EXPERTS * SPLIT, MODEL_WIDTH, H_DEV)
    return dx.reshape(TOKENS, MODEL_WIDTH), total[0], total[1], total[2]
```

```python
import jax
import jax.numpy as jnp
from jax import lax
from jax.sharding import Mesh
from jax.sharding import PartitionSpec as P

WINDOW_EXPERTS = 4
SPLIT = 8
PAD = 128


def route_columns(expert_index, slot, gate):
    experts = jnp.arange(PAD, dtype=jnp.int32)
    hit = (expert_index[:, :, None] == experts) & (slot >= 0)[:, :, None]
    live = jnp.sum(hit.astype(jnp.float32), axis=1)
    weight = jnp.sum(jnp.where(hit, gate[:, :, None].astype(jnp.float32), 0.0), axis=1)
    return live.astype(jnp.bfloat16), weight.astype(jnp.bfloat16)


def local(tokens, out_grad, expert_index, slot, gate, w_gate, w_up, w_down):
    tok, width = tokens.shape
    n_yl, n_z = lax.axis_size("yl"), lax.axis_size("z")
    sources = n_yl * n_z
    n_yh, n_x, n_core = lax.axis_size("yh"), lax.axis_size("x"), lax.axis_size("core")
    hidden = w_gate.shape[2]
    expert = (lax.axis_index("yl") * n_z + lax.axis_index("z")) // SPLIT

    weights = jnp.concatenate([w_gate[0], w_up[0], w_down[0]], axis=1)
    weights_pad = jnp.pad(weights, ((0, PAD), (0, 0)))

    live, weight = route_columns(expert_index, slot, gate)
    send = jnp.concatenate(
        [
            jnp.concatenate([tokens, live], axis=1),
            jnp.concatenate([out_grad, weight], axis=1),
        ],
        axis=0,
    )
    rows = lax.all_gather(send, ("yl", "z"), axis=0, tiled=True)

    mine = (jnp.arange(PAD, dtype=jnp.int32) == expert).astype(jnp.float32)
    routes = jnp.sum(rows[:, width:].astype(jnp.float32) * mine, axis=1)
    routes = routes.reshape(sources, 2, tok, 1)
    live_rows, gate_rows = routes[:, 0], routes[:, 1]

    act = jnp.dot(rows, weights_pad, preferred_element_type=jnp.float32)
    act = act.reshape(sources, 2, tok, 3 * hidden)
    act_a = act[:, 0, :, :hidden]
    act_b = act[:, 0, :, hidden : 2 * hidden]
    grad_h = act[:, 1, :, 2 * hidden :] * gate_rows
    sig = jax.nn.sigmoid(act_a)
    silu = act_a * sig
    is_live = live_rows > 0
    hid = jnp.where(is_live, silu * act_b * gate_rows, 0.0).astype(jnp.bfloat16)
    grad_a = jnp.where(is_live, grad_h * act_b * sig * (1.0 + act_a * (1.0 - sig)), 0.0)
    grad_b = jnp.where(is_live, grad_h * silu, 0.0)
    grad_ab = jnp.concatenate([grad_a, grad_b], axis=2).astype(jnp.bfloat16)

    by_z = grad_ab.reshape(n_yl, n_z, tok, 2 * hidden).transpose(1, 0, 2, 3)
    back = lax.dot_general(
        by_z.reshape(sources * tok, 2 * hidden),
        weights[:, : 2 * hidden],
        (((1,), (1,)), ((), ())),
        preferred_element_type=jnp.float32,
    ).astype(jnp.bfloat16)
    back = lax.psum_scatter(back, "z", scatter_dimension=0, tiled=True)
    input_grad = lax.psum_scatter(back, "yl", scatter_dimension=0, tiled=True)

    upper = jnp.concatenate([grad_ab, jnp.zeros_like(hid)], axis=2)
    lower = jnp.concatenate([jnp.zeros_like(grad_ab), hid], axis=2)
    both = jnp.stack([upper, lower], axis=1).reshape(sources * 2 * tok, 3 * hidden)
    grads = lax.dot_general(
        rows[:, :width], both, (((0,), (0,)), ((), ())), preferred_element_type=jnp.float32
    ).astype(jnp.bfloat16)
    grads = grads.reshape(n_yh, n_x, n_core, -1, 3 * hidden).transpose(2, 1, 0, 3, 4)
    grads = grads.reshape(width, 3 * hidden)
    grads = lax.psum_scatter(grads, "core", scatter_dimension=0, tiled=True)
    grads = lax.psum_scatter(grads, "x", scatter_dimension=0, tiled=True)
    grads = lax.psum_scatter(grads, "yh", scatter_dimension=0, tiled=True)
    return (
        input_grad,
        grads[None, :, :hidden],
        grads[None, :, hidden : 2 * hidden],
        grads[None, :, 2 * hidden :],
    )


def solution(mesh):
    fine = Mesh(mesh.devices.reshape(2, 4, 2, 2, 16), ("yh", "x", "core", "yl", "z"))
    every = P(("yh", "x", "core", "yl", "z"), None)
    slices = P(("yl", "z"), None, None)
    grads = P(("yl", "z"), ("yh", "x", "core"), None)
    return jax.shard_map(
        local,
        mesh=fine,
        in_specs=(every, every, every, every, every, slices, slices, slices),
        out_specs=(every, grads, grads, grads),
        check_vma=False,
    )
```

```python
import jax
import jax.numpy as jnp
from jax import lax
from jax.sharding import Mesh
from jax.sharding import PartitionSpec as P

WINDOW_EXPERTS = 4
SPLIT = 8
PAD = 128
SWAP = [(0, 1), (1, 0)]


def route_columns(expert_index, slot, gate):
    experts = jnp.arange(PAD, dtype=jnp.int32)
    hit = (expert_index[:, :, None] == experts) & (slot >= 0)[:, :, None]
    live = jnp.sum(hit.astype(jnp.float32), axis=1)
    weight = jnp.sum(jnp.where(hit, gate[:, :, None].astype(jnp.float32), 0.0), axis=1)
    return live.astype(jnp.bfloat16), weight.astype(jnp.bfloat16)


def add(*terms):
    return sum(t.astype(jnp.float32) for t in terms).astype(jnp.bfloat16)


def take(array, index, axis):
    return lax.dynamic_index_in_dim(array, index, axis, keepdims=False)


def reduce_weights(grads):
    n_yh, n_x, n_core = lax.axis_size("yh"), lax.axis_size("x"), lax.axis_size("core")
    yh, x, core = lax.axis_index("yh"), lax.axis_index("x"), lax.axis_index("core")
    grads = grads.reshape(n_yh * n_x, n_core, -1, grads.shape[1])
    other = lax.ppermute(take(grads, 1 - core, 1), "core", SWAP)
    grads = add(take(grads, core, 1), other)

    grads = grads.reshape(n_yh, n_x, *grads.shape[1:])
    right = [(i, (i + 1) % n_x) for i in range(n_x)]
    left = [(i, (i - 1) % n_x) for i in range(n_x)]
    after = take(grads, (x + 1) % n_x, 1)
    before = take(grads, (x + n_x - 1) % n_x, 1)
    across = take(grads, (x + 2) % n_x, 1)
    own = take(grads, x, 1)
    from_left = lax.ppermute(jnp.stack([across[0], after[1]]), "x", right)
    from_right = lax.ppermute(jnp.stack([across[1], before[0]]), "x", left)
    last_left = lax.ppermute(add(after[0], from_left[0]), "x", right)
    last_right = lax.ppermute(add(before[1], from_right[0]), "x", left)
    low = add(own[0], last_left, from_right[1])
    high = add(own[1], last_right, from_left[1])

    is_low = yh == 0
    other = lax.ppermute(jnp.where(is_low, high, low), "yh", SWAP)
    return add(jnp.where(is_low, low, high), other)


def local(tokens, out_grad, expert_index, slot, gate, w_gate, w_up, w_down):
    tok, width = tokens.shape
    n_yl, n_z = lax.axis_size("yl"), lax.axis_size("z")
    sources = n_yl * n_z
    hidden = w_gate.shape[2]
    expert = (lax.axis_index("yl") * n_z + lax.axis_index("z")) // SPLIT

    weights = jnp.concatenate([w_gate[0], w_up[0], w_down[0]], axis=1)
    weights_pad = lax.optimization_barrier(jnp.pad(weights, ((0, PAD), (0, 0))))

    live, weight = route_columns(expert_index, slot, gate)
    send = jnp.concatenate(
        [
            jnp.concatenate([tokens, live], axis=1),
            jnp.concatenate([out_grad, weight], axis=1),
        ],
        axis=0,
    )
    partner = lax.ppermute(send, "yl", SWAP)
    rows = lax.all_gather(jnp.concatenate([send, partner], axis=0), "z", axis=0, tiled=True)

    mine = (jnp.arange(PAD, dtype=jnp.int32) == expert).astype(jnp.float32)
    routes = jnp.sum(rows[:, width:].astype(jnp.float32) * mine, axis=1)
    routes = routes.reshape(sources, 2, tok, 1)
    live_rows, gate_rows = routes[:, 0], routes[:, 1]

    act = jnp.dot(rows, weights_pad, preferred_element_type=jnp.float32)
    act = act.reshape(sources, 2, tok, 3 * hidden)
    act_a = act[:, 0, :, :hidden]
    act_b = act[:, 0, :, hidden : 2 * hidden]
    grad_h = act[:, 1, :, 2 * hidden :] * gate_rows
    sig = jax.nn.sigmoid(act_a)
    silu = act_a * sig
    is_live = live_rows > 0
    hid = jnp.where(is_live, silu * act_b * gate_rows, 0.0).astype(jnp.bfloat16)
    grad_a = jnp.where(is_live, grad_h * act_b * sig * (1.0 + act_a * (1.0 - sig)), 0.0)
    grad_b = jnp.where(is_live, grad_h * silu, 0.0)
    grad_ab = jnp.concatenate([grad_a, grad_b], axis=2).astype(jnp.bfloat16)

    back = lax.dot_general(
        grad_ab.reshape(sources * tok, 2 * hidden),
        weights[:, : 2 * hidden],
        (((1,), (1,)), ((), ())),
        preferred_element_type=jnp.float32,
    ).astype(jnp.bfloat16)

    upper = jnp.concatenate([grad_ab, jnp.zeros_like(hid)], axis=2)
    lower = jnp.concatenate([jnp.zeros_like(grad_ab), hid], axis=2)
    both = jnp.stack([upper, lower], axis=1).reshape(sources * 2 * tok, 3 * hidden)
    back, both = lax.optimization_barrier((back, both))
    grads = lax.dot_general(
        rows[:, :width], both, (((0,), (0,)), ((), ())), preferred_element_type=jnp.float32
    ).astype(jnp.bfloat16)
    grads = reduce_weights(grads)

    back = lax.psum_scatter(back, "z", scatter_dimension=0, tiled=True)
    input_grad = add(back[:tok], lax.ppermute(back[tok:], "yl", SWAP))
    return (
        input_grad,
        grads[None, :, :hidden],
        grads[None, :, hidden : 2 * hidden],
        grads[None, :, 2 * hidden :],
    )


def solution(mesh):
    fine = Mesh(mesh.devices.reshape(2, 4, 2, 2, 16), ("yh", "x", "core", "yl", "z"))
    every = P(("yh", "x", "core", "yl", "z"), None)
    slices = P(("yl", "z"), None, None)
    grads = P(("yl", "z"), ("yh", "x", "core"), None)
    return jax.shard_map(
        local,
        mesh=fine,
        in_specs=(every, every, every, every, every, slices, slices, slices),
        out_specs=(every, grads, grads, grads),
        check_vma=False,
    )
```

```python
import jax
import jax.numpy as jnp
from jax import lax
from jax.sharding import Mesh
from jax.sharding import PartitionSpec as P

WINDOW_EXPERTS = 4
SPLIT = 8
PAD = 128
SWAP = [(0, 1), (1, 0)]


def route_columns(expert_index, slot, gate):
    experts = jnp.arange(PAD, dtype=jnp.int32)
    hit = (expert_index[:, :, None] == experts) & (slot >= 0)[:, :, None]
    live = jnp.sum(hit.astype(jnp.float32), axis=1)
    weight = jnp.sum(jnp.where(hit, gate[:, :, None].astype(jnp.float32), 0.0), axis=1)
    return live.astype(jnp.bfloat16), weight.astype(jnp.bfloat16)


def add(*terms):
    return sum(t.astype(jnp.float32) for t in terms).astype(jnp.bfloat16)


def take(array, index, axis):
    return lax.dynamic_index_in_dim(array, index, axis, keepdims=False)


def pair_steps(place):
    return [
        [
            (place(p, c), place(p ^ 1 if (c + step) % 2 == 0 else 3 - p, c))
            for p in range(4)
            for c in range(2)
        ]
        for step in range(2)
    ]


X_RING = ("x", "core"), pair_steps(lambda p, c: p * 2 + c)
Y_RING = ("yh", "core", "yl"), pair_steps(lambda p, c: (p // 2 * 2 + c) * 2 + p % 2)


def pair_sum(ring, own, first, second, across):
    axes, (step1, step2) = ring
    got = lax.ppermute(jnp.stack([first, across]), axes, step1)
    last = lax.ppermute(add(second, got[1]), axes, step2)
    return add(own, got[0], last)


def x_blocks(blocks, axis):
    x, core = lax.axis_index("x"), lax.axis_index("core")
    up = (x + core) % 2 == 0
    after, before = (x + 1) % 4, (x + 3) % 4
    first, second = jnp.where(up, after, before), jnp.where(up, before, after)
    return [take(blocks, at, axis) for at in (x, first, second, (x + 2) % 4)]


def y_blocks(blocks):
    yh, even = lax.axis_index("yh"), lax.axis_index("core") == 0
    cols = blocks.shape[-1] // 2
    here, there = take(blocks, yh, 0), take(blocks, 1 - yh, 0)
    near, far = here[..., cols:], there[..., cols:]
    first, second = jnp.where(even, near, far), jnp.where(even, far, near)
    return [here[..., :cols], first, second, there[..., :cols]]


def reduce_weights(grads):
    n_yh, n_x, n_core = lax.axis_size("yh"), lax.axis_size("x"), lax.axis_size("core")
    core = lax.axis_index("core")
    grads = grads.reshape(n_yh * n_x, n_core, -1, grads.shape[1])
    other = lax.ppermute(take(grads, 1 - core, 1), "core", SWAP)
    grads = add(take(grads, core, 1), other)

    cut = grads.shape[1] // 2
    upper = grads[:, :cut].reshape(n_yh, n_x, cut, -1)
    lower = grads[:, cut:].reshape(n_yh, n_x, cut, -1)
    upper = pair_sum(X_RING, *x_blocks(upper, 1))
    lower = pair_sum(Y_RING, *y_blocks(lower))
    upper = pair_sum(Y_RING, *y_blocks(upper))
    lower = pair_sum(X_RING, *x_blocks(lower, 0))
    return jnp.concatenate([upper, lower], axis=0)


def partner_weights(weights):
    core = lax.axis_index("core")
    half = take(weights.reshape(2, -1, weights.shape[1]), core, 0)
    mine = lax.ppermute(half, "yl", SWAP)
    other = lax.ppermute(mine, "core", SWAP)
    first = core == 0
    return jnp.concatenate([jnp.where(first, mine, other), jnp.where(first, other, mine)], axis=0)


def local(tokens, out_grad, expert_index, slot, gate, w_gate, w_up, w_down):
    tok, width = tokens.shape
    n_yl, n_z = lax.axis_size("yl"), lax.axis_size("z")
    hidden = w_gate.shape[2]
    yl, z = lax.axis_index("yl"), lax.axis_index("z")
    experts = [(row * n_z + z) // SPLIT for row in (yl, 1 - yl)]

    live, weight = route_columns(expert_index, slot, gate)
    send = jnp.concatenate(
        [
            jnp.concatenate([tokens, live], axis=1),
            jnp.concatenate([out_grad, weight], axis=1),
        ],
        axis=0,
    )
    rows = lax.all_gather(send, "z", axis=0, tiled=True)

    own = jnp.concatenate([w_gate[0], w_up[0], w_down[0]], axis=1)
    partner = partner_weights(own)
    weights = jnp.concatenate(
        [w[:, i * hidden : (i + 1) * hidden] for i in range(3) for w in (own, partner)], axis=1
    )
    weights = lax.optimization_barrier(jnp.pad(weights, ((0, PAD), (0, 0))))

    columns = jnp.arange(PAD, dtype=jnp.int32)
    routes = rows[:, width:].astype(jnp.float32)
    routes = jnp.concatenate(
        [
            jnp.broadcast_to(
                jnp.sum(jnp.where(columns == e, routes, 0.0), axis=1, keepdims=True),
                (n_z * 2 * tok, hidden),
            )
            for e in experts
        ],
        axis=1,
    ).reshape(n_z, 2, tok, 2 * hidden)
    live_rows, gate_rows = routes[:, 0], routes[:, 1]

    act = jnp.dot(rows, weights, preferred_element_type=jnp.float32)
    act = act.reshape(n_z, 2, tok, 6 * hidden)
    act_a = act[:, 0, :, : 2 * hidden]
    act_b = act[:, 0, :, 2 * hidden : 4 * hidden]
    grad_h = act[:, 1, :, 4 * hidden :] * gate_rows
    sig = jax.nn.sigmoid(act_a)
    silu = act_a * sig
    is_live = live_rows > 0
    hid = jnp.where(is_live, silu * act_b * gate_rows, 0.0).astype(jnp.bfloat16)
    grad_a = jnp.where(is_live, grad_h * act_b * sig * (1.0 + act_a * (1.0 - sig)), 0.0)
    grad_a = grad_a.astype(jnp.bfloat16)
    grad_b = jnp.where(is_live, grad_h * silu, 0.0).astype(jnp.bfloat16)

    zero = jnp.zeros((n_z, tok, hidden), jnp.bfloat16)
    upper, lower = [], []
    for i in range(2):
        cut = slice(i * hidden, (i + 1) * hidden)
        upper += [grad_a[:, :, cut], grad_b[:, :, cut], zero]
        lower += [zero, zero, hid[:, :, cut]]
    both = jnp.stack([jnp.concatenate(upper, axis=2), jnp.concatenate(lower, axis=2)], axis=1)
    both = both.reshape(n_z * 2 * tok, 6 * hidden)
    back = lax.dot_general(
        jnp.concatenate([grad_a, grad_b], axis=2).reshape(n_z * tok, 4 * hidden),
        weights[:width, : 4 * hidden],
        (((1,), (1,)), ((), ())),
        preferred_element_type=jnp.float32,
    ).astype(jnp.bfloat16)
    back, both = lax.optimization_barrier((back, both))
    grads = lax.dot_general(
        rows[:, :width], both, (((0,), (0,)), ((), ())), preferred_element_type=jnp.float32
    ).astype(jnp.bfloat16)
    grads = reduce_weights(grads)
    input_grad = lax.psum_scatter(back, "z", scatter_dimension=0, tiled=True)
    return (
        input_grad,
        grads[None, :, :hidden],
        grads[None, :, hidden : 2 * hidden],
        grads[None, :, 2 * hidden :],
    )


def solution(mesh):
    fine = Mesh(mesh.devices.reshape(2, 4, 2, 2, 16), ("yh", "x", "core", "yl", "z"))
    every = P(("yh", "x", "core", "yl", "z"), None)
    slices = P(("yl", "z"), None, None)
    grads = P(("yl", "z"), ("yh", "x", "core"), None)
    return jax.shard_map(
        local,
        mesh=fine,
        in_specs=(every, every, every, every, every, slices, slices, slices),
        out_specs=(every, grads, grads, grads),
        check_vma=False,
    )
```

```python
import jax
import jax.numpy as jnp
from jax import lax
from jax.experimental import pallas as pl
from jax.experimental.pallas import tpu as pltpu
from jax.sharding import Mesh
from jax.sharding import PartitionSpec as P

WINDOW_EXPERTS = 4
SPLIT = 8
PAD = 128
CHUNKS = 5
VMEM_LIMIT = 60 * 1024 * 1024
SWAP = [(0, 1), (1, 0)]


def flat(block):
    return block.reshape(-1, block.shape[-1])


def forward_kernel(experts, rows, weights, back, dab, hid, rows_v, routes_v, w_v, back_v, total, sems):
    n_z, both, chunk = rows_v.shape[1:]
    tok = both // 2
    hidden = hid.shape[1] // 2

    def row_copy(k):
        return pltpu.make_async_copy(
            rows.at[:, :, pl.ds(pl.multiple_of(k * chunk, 128), chunk)], rows_v.at[k], sems.at[0, k]
        )

    def weight_copy(k):
        return pltpu.make_async_copy(
            weights.at[pl.ds(pl.multiple_of(k * chunk, 128), chunk), :], w_v.at[k], sems.at[1, k]
        )

    def back_copy(k):
        return pltpu.make_async_copy(
            back_v.at[k], back.at[:, pl.ds(pl.multiple_of(k * chunk, 128), chunk)], sems.at[2, k]
        )

    route_copy = pltpu.make_async_copy(
        rows.at[:, :, CHUNKS * chunk : CHUNKS * chunk + PAD], routes_v, sems.at[3, 0]
    )

    def start(k, carry):
        row_copy(k).start()
        weight_copy(k).start()
        return carry

    lax.fori_loop(0, CHUNKS, start, 0)
    route_copy.start()
    total[...] = jnp.zeros_like(total)

    def accumulate(k, carry):
        row_copy(k).wait()
        weight_copy(k).wait()
        x_rows = flat(rows_v[k, :, :tok, :])
        g_rows = flat(rows_v[k, :, tok:, :])
        w = w_v[k]
        total[:, : 4 * hidden] += jnp.dot(
            x_rows, w[:, : 4 * hidden], preferred_element_type=jnp.float32
        )
        total[:, 4 * hidden :] += jnp.dot(
            g_rows, w[:, 4 * hidden :], preferred_element_type=jnp.float32
        )
        return carry

    lax.fori_loop(0, CHUNKS, accumulate, 0)
    route_copy.wait()

    live_rows = flat(routes_v[:, :tok, :]).astype(jnp.float32)
    gate_rows = flat(routes_v[:, tok:, :]).astype(jnp.float32)
    lanes = lax.broadcasted_iota(jnp.int32, live_rows.shape, 1)
    for i in range(2):
        mine = lanes == experts[i]
        live = jnp.sum(jnp.where(mine, live_rows, 0.0), axis=1, keepdims=True) > 0
        gate = jnp.sum(jnp.where(mine, gate_rows, 0.0), axis=1, keepdims=True)
        at = 2 * i * hidden
        act_a = total[:, at : at + hidden]
        act_b = total[:, at + hidden : at + 2 * hidden]
        grad_h = total[:, (4 + i) * hidden : (5 + i) * hidden] * gate
        sig = 1.0 / (1.0 + jnp.exp(-act_a))
        silu = act_a * sig
        grad_a = grad_h * act_b * sig * (1.0 + act_a * (1.0 - sig))
        dab[:, at : at + hidden] = jnp.where(live, grad_a, 0.0).astype(dab.dtype)
        dab[:, at + hidden : at + 2 * hidden] = jnp.where(live, grad_h * silu, 0.0).astype(dab.dtype)
        hid[:, i * hidden : (i + 1) * hidden] = jnp.where(live, silu * act_b * gate, 0.0).astype(
            hid.dtype
        )

    def produce(k, carry):
        back_v[k] = lax.dot_general(
            dab[...],
            w_v[k, :, : 4 * hidden],
            (((1,), (1,)), ((), ())),
            preferred_element_type=jnp.float32,
        ).astype(back_v.dtype)
        back_copy(k).start()
        return carry

    lax.fori_loop(0, CHUNKS, produce, 0)

    def finish(k, carry):
        back_copy(k).wait()
        return carry

    lax.fori_loop(0, CHUNKS, finish, 0)


def forward(experts, rows, weights):
    n_z, both, padded = rows.shape
    width, cols = weights.shape
    hidden, chunk, count = cols // 6, width // CHUNKS, n_z * both // 2
    bf16 = jnp.bfloat16
    vmem = pl.BlockSpec(memory_space=pltpu.VMEM)
    hbm = pl.BlockSpec(memory_space=pl.ANY)
    return pl.pallas_call(
        forward_kernel,
        out_shape=(
            jax.ShapeDtypeStruct((count, width), bf16),
            jax.ShapeDtypeStruct((count, 4 * hidden), bf16),
            jax.ShapeDtypeStruct((count, 2 * hidden), bf16),
        ),
        in_specs=[pl.BlockSpec(memory_space=pltpu.SMEM), hbm, hbm],
        out_specs=(hbm, vmem, vmem),
        scratch_shapes=[
            pltpu.VMEM((CHUNKS, n_z, both, chunk), bf16),
            pltpu.VMEM((n_z, both, PAD), bf16),
            pltpu.VMEM((CHUNKS, chunk, cols), bf16),
            pltpu.VMEM((CHUNKS, count, chunk), bf16),
            pltpu.VMEM((count, cols), jnp.float32),
            pltpu.SemaphoreType.DMA((4, CHUNKS)),
        ],
        compiler_params=pltpu.CompilerParams(vmem_limit_bytes=VMEM_LIMIT),
        cost_estimate=pl.CostEstimate(
            flops=2 * count * width * 10 * hidden, bytes_accessed=16_000_000, transcendentals=0
        ),
    )(experts, rows, weights)


def grads_kernel(part, rows, dab, hid, out):
    tok = rows.shape[1] // 2
    hidden = hid.shape[1] // 2
    count, height, _ = out.shape
    reach = -(-height // 128) * 128

    def product(block, left):
        return lax.dot_general(
            flat(block), left, (((0,), (0,)), ((), ())), preferred_element_type=jnp.float32
        ).astype(out.dtype)

    def write(start, skip):
        for n in range(count):
            at = 2 * height * n + start
            from_x = product(rows[:, :tok, at : at + reach], dab[...])
            from_g = product(rows[:, tok:, at : at + reach], hid[...])
            for i in range(2):
                col = 3 * i * hidden
                out[n, :, col : col + 2 * hidden] = from_x[
                    skip : skip + height, 2 * i * hidden : 2 * (i + 1) * hidden
                ]
                out[n, :, col + 2 * hidden : col + 3 * hidden] = from_g[
                    skip : skip + height, i * hidden : (i + 1) * hidden
                ]

    @pl.when(part[0] == 0)
    def _():
        write(0, 0)

    @pl.when(part[0] == 1)
    def _():
        write(2 * height - reach, reach - height)


def weight_grads(part, rows, dab, hid, steps=4, per_step=2):
    n_z, both, padded = rows.shape
    height = (padded - PAD) // (2 * steps * per_step)
    count, cols = dab.shape[0], dab.shape[1] + hid.shape[1]
    return pl.pallas_call(
        grads_kernel,
        grid_spec=pltpu.PrefetchScalarGridSpec(
            num_scalar_prefetch=1,
            grid=(steps,),
            in_specs=[
                pl.BlockSpec((n_z, both, 2 * height * per_step), lambda i, part: (0, 0, i)),
                pl.BlockSpec(dab.shape, lambda i, part: (0, 0)),
                pl.BlockSpec(hid.shape, lambda i, part: (0, 0)),
            ],
            out_specs=pl.BlockSpec((per_step, height, cols), lambda i, part: (i, 0, 0)),
        ),
        out_shape=jax.ShapeDtypeStruct((steps * per_step, height, cols), jnp.bfloat16),
        compiler_params=pltpu.CompilerParams(vmem_limit_bytes=VMEM_LIMIT),
        cost_estimate=pl.CostEstimate(
            flops=count * (padded - PAD) * cols, bytes_accessed=9_000_000, transcendentals=0
        ),
    )(jnp.reshape(part, (1,)).astype(jnp.int32), rows, dab, hid)


def split_kernel(place, keep_a, got_a, keep_b, got_b, out_a, out_b):
    out_a[...] = add(keep_a[...], got_a[...])[None]
    out_b[...] = add(keep_b[...], got_b[...])[None]


def core_sum(keep, got, slots):
    x, core, yh = lax.axis_index("x"), lax.axis_index("core"), lax.axis_index("yh")
    blocks, part, cols = keep.shape
    n_x, half, cut = blocks // 2, cols // 2, part // 2
    up = (x + core) % 2 == 0
    after, before = (x + 1) % 4, (x + 3) % 4
    a_slots = [x, jnp.where(up, after, before), jnp.where(up, before, after), (x + 2) % 4]
    far = jnp.where(core == 0, 1 - yh, yh)
    b_slots = [(yh, 0), (1 - far, 1), (far, 1), (1 - yh, 0)]
    place = [h * n_x + a_slots[s] for s in slots for h in range(2)]
    place += [h * 2 + m for h, _ in [b_slots[s] for s in slots] for m in range(2)]
    place += [c for _, c in [b_slots[s] for s in slots] for m in range(2)]
    place = jnp.stack([jnp.asarray(v, jnp.int32) for v in place])

    in_a = pl.BlockSpec((1, cut, cols), lambda j, p: (p[j], 0, 0))
    in_b = pl.BlockSpec((2, cut, half), lambda j, p: (p[4 + j], 1, p[8 + j]))

    def out(j, p):
        return (j // 2, j % 2, 0, 0)

    return pl.pallas_call(
        split_kernel,
        grid_spec=pltpu.PrefetchScalarGridSpec(
            num_scalar_prefetch=1,
            grid=(4,),
            in_specs=[in_a, in_a, in_b, in_b],
            out_specs=[
                pl.BlockSpec((1, 1, cut, cols), out),
                pl.BlockSpec((1, 2, cut, half), out),
            ],
        ),
        out_shape=[
            jax.ShapeDtypeStruct((2, 2, cut, cols), keep.dtype),
            jax.ShapeDtypeStruct((2, n_x, cut, half), keep.dtype),
        ],
        compiler_params=pltpu.CompilerParams(vmem_limit_bytes=VMEM_LIMIT),
        cost_estimate=pl.CostEstimate(flops=0, bytes_accessed=6_000_000, transcendentals=0),
    )(place, keep, got, keep, got)


def route_columns(expert_index, slot, gate):
    experts = jnp.arange(PAD, dtype=jnp.int32)
    hit = (expert_index[:, :, None] == experts) & (slot >= 0)[:, :, None]
    live = jnp.sum(hit.astype(jnp.float32), axis=1)
    weight = jnp.sum(jnp.where(hit, gate[:, :, None].astype(jnp.float32), 0.0), axis=1)
    return live.astype(jnp.bfloat16), weight.astype(jnp.bfloat16)


def add(*terms):
    return sum(t.astype(jnp.float32) for t in terms).astype(jnp.bfloat16)


def take(array, index, axis):
    return lax.dynamic_index_in_dim(array, index, axis, keepdims=False)


def pair_steps(place):
    return [
        [
            (place(p, c), place(p ^ 1 if (c + step) % 2 == 0 else 3 - p, c))
            for p in range(4)
            for c in range(2)
        ]
        for step in range(2)
    ]


X_RING = ("x", "core"), pair_steps(lambda p, c: p * 2 + c)
Y_RING = ("yh", "core", "yl"), pair_steps(lambda p, c: (p // 2 * 2 + c) * 2 + p % 2)


def pair_sum(ring, own, second, send):
    axes, (step1, step2) = ring
    got = lax.ppermute(send, axes, step1)
    last = lax.ppermute(add(second, got[1]), axes, step2)
    return add(own, got[0], last)


def x_blocks(blocks, axis):
    x, core = lax.axis_index("x"), lax.axis_index("core")
    up = (x + core) % 2 == 0
    after, before = (x + 1) % 4, (x + 3) % 4
    first, second = jnp.where(up, after, before), jnp.where(up, before, after)
    own, first, second, across = [take(blocks, at, axis) for at in (x, first, second, (x + 2) % 4)]
    return own, second, jnp.stack([first, across])


def y_blocks(blocks):
    yh, even = lax.axis_index("yh"), lax.axis_index("core") == 0
    cols = blocks.shape[-1] // 2
    here, there = take(blocks, yh, 0), take(blocks, 1 - yh, 0)
    near, far = here[..., cols:], there[..., cols:]
    first, second = jnp.where(even, near, far), jnp.where(even, far, near)
    return here[..., :cols], second, jnp.stack([first, there[..., :cols]])


def reduce_weights(rows, dab, hid):
    core = lax.axis_index("core")
    got = lax.ppermute(weight_grads(1 - core, rows, dab, hid), "core", SWAP)
    keep = weight_grads(core, rows, dab, hid)
    send_a, send_b = core_sum(keep, got, (1, 3))
    own_a, own_b = core_sum(keep, got, (0, 2))
    upper = pair_sum(X_RING, own_a[0], own_a[1], send_a)
    lower = pair_sum(Y_RING, own_b[0], own_b[1], send_b)
    upper = pair_sum(Y_RING, *y_blocks(upper))
    lower = pair_sum(X_RING, *x_blocks(lower, 0))
    return jnp.concatenate([upper, lower], axis=0)


def partner_weights(weights):
    core = lax.axis_index("core")
    half = take(weights.reshape(2, -1, weights.shape[1]), core, 0)
    mine = lax.ppermute(half, "yl", SWAP)
    other = lax.ppermute(mine, "core", SWAP)
    first = core == 0
    return jnp.concatenate([jnp.where(first, mine, other), jnp.where(first, other, mine)], axis=0)


def local(tokens, out_grad, expert_index, slot, gate, w_gate, w_up, w_down):
    tok, width = tokens.shape
    n_yl, n_z = lax.axis_size("yl"), lax.axis_size("z")
    hidden = w_gate.shape[2]
    yl, z = lax.axis_index("yl"), lax.axis_index("z")
    experts = [(row * n_z + z) // SPLIT for row in (yl, 1 - yl)]

    live, weight = route_columns(expert_index, slot, gate)
    send = jnp.concatenate(
        [
            jnp.concatenate([tokens, live], axis=1),
            jnp.concatenate([out_grad, weight], axis=1),
        ],
        axis=0,
    )
    rows = lax.all_gather(send, "z", axis=0, tiled=True)

    own = jnp.concatenate([w_gate[0], w_up[0], w_down[0]], axis=1)
    partner = partner_weights(own)
    pairs = 2 * hidden
    weights = jnp.concatenate(
        [own[:, :pairs], partner[:, :pairs], own[:, pairs:], partner[:, pairs:]], axis=1
    )

    rows = rows.reshape(n_z, 2 * tok, width + PAD)
    back, dab, hid = forward(jnp.stack(experts).astype(jnp.int32), rows, weights)
    grads = reduce_weights(rows, dab, hid)
    input_grad = lax.psum_scatter(back, "z", scatter_dimension=0, tiled=True)
    return (
        input_grad,
        grads[None, :, :hidden],
        grads[None, :, hidden : 2 * hidden],
        grads[None, :, 2 * hidden :],
    )


def solution(mesh):
    fine = Mesh(mesh.devices.reshape(2, 4, 2, 2, 16), ("yh", "x", "core", "yl", "z"))
    every = P(("yh", "x", "core", "yl", "z"), None)
    slices = P(("yl", "z"), None, None)
    grads = P(("yl", "z"), ("yh", "x", "core"), None)
    return jax.shard_map(
        local,
        mesh=fine,
        in_specs=(every, every, every, every, every, slices, slices, slices),
        out_specs=(every, grads, grads, grads),
        check_vma=False,
    )
```

```python
import jax
import jax.numpy as jnp
from jax import lax
from jax.experimental import pallas as pl
from jax.experimental.pallas import tpu as pltpu
from jax.sharding import Mesh
from jax.sharding import PartitionSpec as P

WINDOW_EXPERTS = 4
SPLIT = 8
PAD = 128
CHUNKS = 5
BLOCKS = 8
VMEM_LIMIT = 60 * 1024 * 1024
SWAP = [(0, 1), (1, 0)]


def flat(block):
    return block.reshape(-1, block.shape[-1])


def dot_rows(block, other):
    return lax.dot_general(
        flat(block), other, (((0,), (0,)), ((), ())), preferred_element_type=jnp.float32
    ).astype(jnp.bfloat16)


def put_grads(out, rows, at, skip, dab, hid):
    height, tok, hidden = out.shape[0], rows.shape[1] // 2, hid.shape[1] // 2
    reach = -(-height // 128) * 128
    columns = pl.ds(at, reach)
    from_x = dot_rows(rows[:, :tok, columns], dab[...])
    from_g = dot_rows(rows[:, tok:, columns], hid[...])
    fill_grads(out, from_x, from_g, skip, hidden)


def fill_grads(out, from_x, from_g, skip, hidden):
    height = out.shape[0]
    for i in range(2):
        col = 3 * i * hidden
        out[:, col : col + 2 * hidden] = from_x[
            skip : skip + height, 2 * i * hidden : 2 * (i + 1) * hidden
        ]
        out[:, col + 2 * hidden : col + 3 * hidden] = from_g[
            skip : skip + height, i * hidden : (i + 1) * hidden
        ]


def each_half(part, height, body):
    reach = -(-height // 128) * 128

    @pl.when(part == 0)
    def _():
        body(0, 0)

    @pl.when(part == 1)
    def _():
        body(2 * height - reach, reach - height)


def forward_kernel(
    scalars, rows, weights, back, dab, hid, send, rows_v, turned, w_v, back_v, send_v, total, sems
):
    n_z, both, _ = rows_v.shape
    chunk = w_v.shape[1]
    tok = both // 2
    hidden, bf16 = hid.shape[1] // 2, jnp.bfloat16
    width = CHUNKS * chunk
    blocks, height, _ = send_v.shape

    def columns(k):
        return pl.ds(pl.multiple_of(k * chunk, 128), chunk)

    def row_copy(k):
        at = columns(k)
        return pltpu.make_async_copy(rows.at[:, :, at], rows_v.at[:, :, at], sems.at[0, k])

    def weight_copy(k):
        return pltpu.make_async_copy(weights.at[columns(k), :], w_v.at[k], sems.at[1, k])

    def back_copy(k):
        return pltpu.make_async_copy(back_v.at[k], back.at[:, columns(k)], sems.at[2, k])

    def send_copy(n):
        return pltpu.make_async_copy(send_v.at[n], send.at[n], sems.at[3, n])

    last = pl.ds(width, PAD)
    route_copy = pltpu.make_async_copy(rows.at[:, :, last], rows_v.at[:, :, last], sems.at[4, 0])

    for k in range(CHUNKS):
        row_copy(k).start()
        weight_copy(k).start()
    route_copy.start()

    for k in range(CHUNKS):
        row_copy(k).wait()
        weight_copy(k).wait()
        at = slice(k * chunk, (k + 1) * chunk)
        x_rows, g_rows = flat(rows_v[:, :tok, at]), flat(rows_v[:, tok:, at])
        turned[0, at, :] = x_rows.T
        turned[1, at, :] = g_rows.T
        from_x = jnp.dot(x_rows, w_v[k, :, : 4 * hidden], preferred_element_type=jnp.float32)
        from_g = jnp.dot(g_rows, w_v[k, :, 4 * hidden :], preferred_element_type=jnp.float32)
        if k == 0:
            total[:, : 4 * hidden] = from_x
            total[:, 4 * hidden :] = from_g
        else:
            total[:, : 4 * hidden] += from_x
            total[:, 4 * hidden :] += from_g
    route_copy.wait()

    live_rows = flat(rows_v[:, :tok, width:]).astype(jnp.float32)
    gate_rows = flat(rows_v[:, tok:, width:]).astype(jnp.float32)
    lanes = lax.broadcasted_iota(jnp.int32, live_rows.shape, 1)
    for i in range(2):
        mine = lanes == scalars[i]
        live = jnp.sum(jnp.where(mine, live_rows, 0.0), axis=1, keepdims=True) > 0
        gate = jnp.sum(jnp.where(mine, gate_rows, 0.0), axis=1, keepdims=True)
        at = 2 * i * hidden
        act_a = total[:, at : at + hidden]
        act_b = total[:, at + hidden : at + 2 * hidden]
        grad_h = total[:, (4 + i) * hidden : (5 + i) * hidden] * gate
        sig = 1.0 / (1.0 + jnp.exp(-act_a))
        silu = act_a * sig
        grad_a = grad_h * act_b * sig * (1.0 + act_a * (1.0 - sig))
        dab[:, at : at + hidden] = jnp.where(live, grad_a, 0.0).astype(dab.dtype)
        dab[:, at + hidden : at + 2 * hidden] = jnp.where(live, grad_h * silu, 0.0).astype(dab.dtype)
        hid[:, i * hidden : (i + 1) * hidden] = jnp.where(live, silu * act_b * gate, 0.0).astype(
            hid.dtype
        )

    for k in range(CHUNKS):
        back_v[k] = lax.dot_general(
            dab[...],
            w_v[k, :, : 4 * hidden],
            (((1,), (1,)), ((), ())),
            preferred_element_type=jnp.float32,
        ).astype(back_v.dtype)
        back_copy(k).start()

    for n in range(blocks):
        at = pl.ds(pl.multiple_of((2 * n + scalars[2]) * height, 64), height)
        from_x = jnp.dot(turned[0, at, :], dab[...], preferred_element_type=jnp.float32)
        from_g = jnp.dot(turned[1, at, :], hid[...], preferred_element_type=jnp.float32)
        fill_grads(send_v.at[n], from_x.astype(bf16), from_g.astype(bf16), 0, hidden)
        send_copy(n).start()
    for k in range(CHUNKS):
        back_copy(k).wait()
    for n in range(blocks):
        send_copy(n).wait()


def forward(scalars, rows, weights):
    n_z, both, padded = rows.shape
    width, cols = weights.shape
    hidden, chunk, count = cols // 6, width // CHUNKS, n_z * both // 2
    height = width // (2 * BLOCKS)
    bf16 = jnp.bfloat16
    vmem = pl.BlockSpec(memory_space=pltpu.VMEM)
    hbm = pl.BlockSpec(memory_space=pl.ANY)
    return pl.pallas_call(
        forward_kernel,
        out_shape=(
            jax.ShapeDtypeStruct((count, width), bf16),
            jax.ShapeDtypeStruct((count, 4 * hidden), bf16),
            jax.ShapeDtypeStruct((count, 2 * hidden), bf16),
            jax.ShapeDtypeStruct((BLOCKS, height, cols), bf16),
        ),
        in_specs=[pl.BlockSpec(memory_space=pltpu.SMEM), hbm, hbm],
        out_specs=(hbm, vmem, vmem, hbm),
        scratch_shapes=[
            pltpu.VMEM((n_z, both, padded), bf16),
            pltpu.VMEM((2, width, count), bf16),
            pltpu.VMEM((CHUNKS, chunk, cols), bf16),
            pltpu.VMEM((CHUNKS, count, chunk), bf16),
            pltpu.VMEM((BLOCKS, height, cols), bf16),
            pltpu.VMEM((count, cols), jnp.float32),
            pltpu.SemaphoreType.DMA((5, BLOCKS)),
        ],
        compiler_params=pltpu.CompilerParams(vmem_limit_bytes=VMEM_LIMIT),
        cost_estimate=pl.CostEstimate(
            flops=2 * count * width * 14 * hidden, bytes_accessed=20_000_000, transcendentals=0
        ),
    )(scalars, rows, weights)


def grads_kernel(part, rows, dab, hid, out):
    count, height, _ = out.shape

    def half(start, skip):
        for n in range(count):
            put_grads(out.at[n], rows, 2 * height * n + start, skip, dab, hid)

    each_half(part[0], height, half)


def weight_grads(part, rows, dab, hid, per_step=2):
    n_z, both, padded = rows.shape
    height = (padded - PAD) // (2 * BLOCKS)
    count, cols = dab.shape[0], dab.shape[1] + hid.shape[1]
    return pl.pallas_call(
        grads_kernel,
        grid_spec=pltpu.PrefetchScalarGridSpec(
            num_scalar_prefetch=1,
            grid=(BLOCKS // per_step,),
            in_specs=[
                pl.BlockSpec((n_z, both, 2 * height * per_step), lambda i, part: (0, 0, i)),
                pl.BlockSpec(dab.shape, lambda i, part: (0, 0)),
                pl.BlockSpec(hid.shape, lambda i, part: (0, 0)),
            ],
            out_specs=pl.BlockSpec((per_step, height, cols), lambda i, part: (i, 0, 0)),
        ),
        out_shape=jax.ShapeDtypeStruct((BLOCKS, height, cols), jnp.bfloat16),
        compiler_params=pltpu.CompilerParams(vmem_limit_bytes=VMEM_LIMIT),
        cost_estimate=pl.CostEstimate(
            flops=count * (padded - PAD) * cols, bytes_accessed=9_000_000, transcendentals=0
        ),
    )(jnp.reshape(part, (1,)).astype(jnp.int32), rows, dab, hid)


def split_kernel(place, keep_a, got_a, keep_b, got_b, out_a, out_b):
    out_a[...] = add(keep_a[...], got_a[...])[None]
    out_b[...] = add(keep_b[...], got_b[...])[None]


def core_sum(keep, got, slots):
    x, core, yh = lax.axis_index("x"), lax.axis_index("core"), lax.axis_index("yh")
    blocks, part, cols = keep.shape
    n_x, half, cut = blocks // 2, cols // 2, part // 2
    up = (x + core) % 2 == 0
    after, before = (x + 1) % 4, (x + 3) % 4
    a_slots = [x, jnp.where(up, after, before), jnp.where(up, before, after), (x + 2) % 4]
    far = jnp.where(core == 0, 1 - yh, yh)
    b_slots = [(yh, 0), (1 - far, 1), (far, 1), (1 - yh, 0)]
    place = [h * n_x + a_slots[s] for s in slots for h in range(2)]
    place += [h * 2 + m for h, _ in [b_slots[s] for s in slots] for m in range(2)]
    place += [c for _, c in [b_slots[s] for s in slots] for m in range(2)]
    place = jnp.stack([jnp.asarray(v, jnp.int32) for v in place])

    in_a = pl.BlockSpec((1, cut, cols), lambda j, p: (p[j], 0, 0))
    in_b = pl.BlockSpec((2, cut, half), lambda j, p: (p[4 + j], 1, p[8 + j]))

    def out(j, p):
        return (j // 2, j % 2, 0, 0)

    return pl.pallas_call(
        split_kernel,
        grid_spec=pltpu.PrefetchScalarGridSpec(
            num_scalar_prefetch=1,
            grid=(4,),
            in_specs=[in_a, in_a, in_b, in_b],
            out_specs=[
                pl.BlockSpec((1, 1, cut, cols), out),
                pl.BlockSpec((1, 2, cut, half), out),
            ],
        ),
        out_shape=[
            jax.ShapeDtypeStruct((2, 2, cut, cols), keep.dtype),
            jax.ShapeDtypeStruct((2, n_x, cut, half), keep.dtype),
        ],
        compiler_params=pltpu.CompilerParams(vmem_limit_bytes=VMEM_LIMIT),
        cost_estimate=pl.CostEstimate(flops=0, bytes_accessed=6_000_000, transcendentals=0),
    )(place, keep, got, keep, got)


def route_columns(expert_index, slot, gate):
    experts = jnp.arange(PAD, dtype=jnp.int32)
    hit = (expert_index[:, :, None] == experts) & (slot >= 0)[:, :, None]
    live = jnp.sum(hit.astype(jnp.float32), axis=1)
    weight = jnp.sum(jnp.where(hit, gate[:, :, None].astype(jnp.float32), 0.0), axis=1)
    return live.astype(jnp.bfloat16), weight.astype(jnp.bfloat16)


def add(*terms):
    return sum(t.astype(jnp.float32) for t in terms).astype(jnp.bfloat16)


def take(array, index, axis):
    return lax.dynamic_index_in_dim(array, index, axis, keepdims=False)


def pair_steps(place):
    return [
        [
            (place(p, c), place(p ^ 1 if (c + step) % 2 == 0 else 3 - p, c))
            for p in range(4)
            for c in range(2)
        ]
        for step in range(2)
    ]


X_RING = ("x", "core"), pair_steps(lambda p, c: p * 2 + c)
Y_RING = ("yh", "core", "yl"), pair_steps(lambda p, c: (p // 2 * 2 + c) * 2 + p % 2)


def pair_sum(ring, own, second, send):
    axes, (step1, step2) = ring
    got = lax.ppermute(send, axes, step1)
    last = lax.ppermute(add(second, got[1]), axes, step2)
    return add(own, got[0], last)


def x_blocks(blocks, axis):
    x, core = lax.axis_index("x"), lax.axis_index("core")
    up = (x + core) % 2 == 0
    after, before = (x + 1) % 4, (x + 3) % 4
    first, second = jnp.where(up, after, before), jnp.where(up, before, after)
    own, first, second, across = [take(blocks, at, axis) for at in (x, first, second, (x + 2) % 4)]
    return own, second, jnp.stack([first, across])


def y_blocks(blocks):
    yh, even = lax.axis_index("yh"), lax.axis_index("core") == 0
    cols = blocks.shape[-1] // 2
    here, there = take(blocks, yh, 0), take(blocks, 1 - yh, 0)
    near, far = here[..., cols:], there[..., cols:]
    first, second = jnp.where(even, near, far), jnp.where(even, far, near)
    return here[..., :cols], second, jnp.stack([first, there[..., :cols]])


def reduce_weights(send, rows, dab, hid):
    core = lax.axis_index("core")
    got = lax.ppermute(send, "core", SWAP)
    keep = weight_grads(core, rows, dab, hid)
    send_a, send_b = core_sum(keep, got, (1, 3))
    own_a, own_b = core_sum(keep, got, (0, 2))
    upper = pair_sum(X_RING, own_a[0], own_a[1], send_a)
    lower = pair_sum(Y_RING, own_b[0], own_b[1], send_b)
    upper = pair_sum(Y_RING, *y_blocks(upper))
    lower = pair_sum(X_RING, *x_blocks(lower, 0))
    return jnp.concatenate([upper, lower], axis=0)


def partner_weights(weights):
    core = lax.axis_index("core")
    half = take(weights.reshape(2, -1, weights.shape[1]), core, 0)
    mine = lax.ppermute(half, "yl", SWAP)
    other = lax.ppermute(mine, "core", SWAP)
    first = core == 0
    return jnp.concatenate([jnp.where(first, mine, other), jnp.where(first, other, mine)], axis=0)


def local(tokens, out_grad, expert_index, slot, gate, w_gate, w_up, w_down):
    tok, width = tokens.shape
    n_yl, n_z = lax.axis_size("yl"), lax.axis_size("z")
    hidden = w_gate.shape[2]
    yl, z = lax.axis_index("yl"), lax.axis_index("z")
    experts = [(row * n_z + z) // SPLIT for row in (yl, 1 - yl)]

    live, weight = route_columns(expert_index, slot, gate)
    send = jnp.concatenate(
        [
            jnp.concatenate([tokens, live], axis=1),
            jnp.concatenate([out_grad, weight], axis=1),
        ],
        axis=0,
    )
    rows = lax.all_gather(send, "z", axis=0, tiled=True)

    own = jnp.concatenate([w_gate[0], w_up[0], w_down[0]], axis=1)
    partner = partner_weights(own)
    pairs = 2 * hidden
    weights = jnp.concatenate(
        [own[:, :pairs], partner[:, :pairs], own[:, pairs:], partner[:, pairs:]], axis=1
    )

    rows = rows.reshape(n_z, 2 * tok, width + PAD)
    scalars = jnp.stack([*experts, 1 - lax.axis_index("core")]).astype(jnp.int32)
    back, dab, hid, send_grads = forward(scalars, rows, weights)
    grads = reduce_weights(send_grads, rows, dab, hid)
    input_grad = lax.psum_scatter(back, "z", scatter_dimension=0, tiled=True)
    return (
        input_grad,
        grads[None, :, :hidden],
        grads[None, :, hidden : 2 * hidden],
        grads[None, :, 2 * hidden :],
    )


def solution(mesh):
    fine = Mesh(mesh.devices.reshape(2, 4, 2, 2, 16), ("yh", "x", "core", "yl", "z"))
    every = P(("yh", "x", "core", "yl", "z"), None)
    slices = P(("yl", "z"), None, None)
    grads = P(("yl", "z"), ("yh", "x", "core"), None)
    return jax.shard_map(
        local,
        mesh=fine,
        in_specs=(every, every, every, every, every, slices, slices, slices),
        out_specs=(every, grads, grads, grads),
        check_vma=False,
    )
```

```python
import jax
import jax.numpy as jnp
from jax import lax
from jax.experimental import pallas as pl
from jax.experimental.pallas import tpu as pltpu
from jax.sharding import Mesh
from jax.sharding import PartitionSpec as P

WINDOW_EXPERTS = 4
SPLIT = 8
PAD = 128
CHUNKS = 5
BLOCKS = 8
VMEM_LIMIT = 60 * 1024 * 1024
SWAP = [(0, 1), (1, 0)]


def flat(block):
    return block.reshape(-1, block.shape[-1])


def dot_f32(block, other):
    return lax.dot_general(
        flat(block), other, (((0,), (0,)), ((), ())), preferred_element_type=jnp.float32
    )


def dot_rows(block, other):
    return dot_f32(block, other).astype(jnp.bfloat16)


def put_grads(out, rows, at, skip, dab, hid):
    height, tok, hidden = out.shape[0], rows.shape[1] // 2, hid.shape[1] // 2
    reach = -(-height // 128) * 128
    columns = pl.ds(at, reach)
    from_x = dot_rows(rows[:, :tok, columns], dab[...])
    from_g = dot_rows(rows[:, tok:, columns], hid[...])
    fill_grads(out, from_x, from_g, skip, hidden)


def fill_grads(out, from_x, from_g, skip, hidden):
    height = out.shape[0]
    for i in range(2):
        col = 3 * i * hidden
        out[:, col : col + 2 * hidden] = from_x[
            skip : skip + height, 2 * i * hidden : 2 * (i + 1) * hidden
        ]
        out[:, col + 2 * hidden : col + 3 * hidden] = from_g[
            skip : skip + height, i * hidden : (i + 1) * hidden
        ]


def each_half(part, height, body):
    reach = -(-height // 128) * 128

    @pl.when(part == 0)
    def _():
        body(0, 0)

    @pl.when(part == 1)
    def _():
        body(2 * height - reach, reach - height)


def forward_kernel(
    scalars, rows, weights, back, dab, hid, swap, rows_v, w_v, back_v, acts_v, total, sems
):
    n_z, both, _ = rows_v.shape
    chunk = w_v.shape[1]
    tok = both // 2
    hidden = hid.shape[1] // 2
    width = CHUNKS * chunk
    blocks, reach = swap.shape[0] - 1, swap.shape[-1]
    step = width // blocks

    def columns(k):
        return pl.ds(pl.multiple_of(k * chunk, 128), chunk)

    def row_copy(k):
        at = columns(k)
        return pltpu.make_async_copy(rows.at[:, :, at], rows_v.at[:, :, at], sems.at[0, k])

    def weight_copy(k):
        return pltpu.make_async_copy(weights.at[columns(k), :], w_v.at[k], sems.at[1, k])

    def back_copy(k):
        return pltpu.make_async_copy(back_v.at[k], back.at[:, columns(k)], sems.at[2, k])

    def swap_copy(n):
        at = pl.ds(pl.multiple_of(n * step + scalars[2] * (step - reach), 128), reach)
        return pltpu.make_async_copy(rows_v.at[:, :, at], swap.at[n], sems.at[3, n])

    acts_copy = pltpu.make_async_copy(acts_v, swap.at[blocks], sems.at[3, blocks])
    last = pl.ds(width, PAD)
    route_copy = pltpu.make_async_copy(rows.at[:, :, last], rows_v.at[:, :, last], sems.at[4, 0])

    for k in range(CHUNKS):
        row_copy(k).start()
        weight_copy(k).start()
    route_copy.start()

    for k in range(CHUNKS):
        row_copy(k).wait()
        weight_copy(k).wait()
        at = slice(k * chunk, (k + 1) * chunk)
        x_rows, g_rows = flat(rows_v[:, :tok, at]), flat(rows_v[:, tok:, at])
        from_x = jnp.dot(x_rows, w_v[k, :, : 4 * hidden], preferred_element_type=jnp.float32)
        from_g = jnp.dot(g_rows, w_v[k, :, 4 * hidden :], preferred_element_type=jnp.float32)
        if k == 0:
            total[:, : 4 * hidden] = from_x
            total[:, 4 * hidden :] = from_g
        else:
            total[:, : 4 * hidden] += from_x
            total[:, 4 * hidden :] += from_g
    route_copy.wait()
    for n in range(blocks):
        swap_copy(n).start()

    live_rows = flat(rows_v[:, :tok, width:]).astype(jnp.float32)
    gate_rows = flat(rows_v[:, tok:, width:]).astype(jnp.float32)
    lanes = lax.broadcasted_iota(jnp.int32, live_rows.shape, 1)
    for i in range(2):
        mine = lanes == scalars[i]
        live = jnp.sum(jnp.where(mine, live_rows, 0.0), axis=1, keepdims=True) > 0
        gate = jnp.sum(jnp.where(mine, gate_rows, 0.0), axis=1, keepdims=True)
        at = 2 * i * hidden
        act_a = total[:, at : at + hidden]
        act_b = total[:, at + hidden : at + 2 * hidden]
        grad_h = total[:, (4 + i) * hidden : (5 + i) * hidden] * gate
        sig = 1.0 / (1.0 + jnp.exp(-act_a))
        silu = act_a * sig
        grad_a = grad_h * act_b * sig * (1.0 + act_a * (1.0 - sig))
        dab[:, at : at + hidden] = jnp.where(live, grad_a, 0.0).astype(dab.dtype)
        dab[:, at + hidden : at + 2 * hidden] = jnp.where(live, grad_h * silu, 0.0).astype(dab.dtype)
        hid[:, i * hidden : (i + 1) * hidden] = jnp.where(live, silu * act_b * gate, 0.0).astype(
            hid.dtype
        )

    edge = 3 * hidden
    acts = jnp.concatenate(
        [dab[:, :edge], jnp.concatenate([dab[:, edge:], hid[...]], axis=1)], axis=0
    )
    acts_v[...] = acts.reshape(acts_v.shape)
    acts_copy.start()

    for k in range(CHUNKS):
        back_v[k] = lax.dot_general(
            dab[...],
            w_v[k, :, : 4 * hidden],
            (((1,), (1,)), ((), ())),
            preferred_element_type=jnp.float32,
        ).astype(back_v.dtype)
        back_copy(k).start()

    for k in range(CHUNKS):
        back_copy(k).wait()
    for n in range(blocks):
        swap_copy(n).wait()
    acts_copy.wait()


def forward(scalars, rows, weights):
    n_z, both, padded = rows.shape
    width, cols = weights.shape
    hidden, chunk, count = cols // 6, width // CHUNKS, n_z * both // 2
    reach = -(-width // (2 * BLOCKS) // 128) * 128
    bf16 = jnp.bfloat16
    vmem = pl.BlockSpec(memory_space=pltpu.VMEM)
    hbm = pl.BlockSpec(memory_space=pl.ANY)
    return pl.pallas_call(
        forward_kernel,
        out_shape=(
            jax.ShapeDtypeStruct((count, width), bf16),
            jax.ShapeDtypeStruct((count, 4 * hidden), bf16),
            jax.ShapeDtypeStruct((count, 2 * hidden), bf16),
            jax.ShapeDtypeStruct((BLOCKS + 1, n_z, both, reach), bf16),
        ),
        in_specs=[pl.BlockSpec(memory_space=pltpu.SMEM), hbm, hbm],
        out_specs=(hbm, vmem, vmem, hbm),
        scratch_shapes=[
            pltpu.VMEM((n_z, both, padded), bf16),
            pltpu.VMEM((CHUNKS, chunk, cols), bf16),
            pltpu.VMEM((CHUNKS, count, chunk), bf16),
            pltpu.VMEM((n_z, both, reach), bf16),
            pltpu.VMEM((count, cols), jnp.float32),
            pltpu.SemaphoreType.DMA((5, BLOCKS + 1)),
        ],
        compiler_params=pltpu.CompilerParams(vmem_limit_bytes=VMEM_LIMIT),
        cost_estimate=pl.CostEstimate(
            flops=2 * count * width * 10 * hidden, bytes_accessed=20_000_000, transcendentals=0
        ),
    )(scalars, rows, weights)


def grads_kernel(part, rows, dab, hid, out):
    count, height, _ = out.shape

    def half(start, skip):
        for n in range(count):
            put_grads(out.at[n], rows, 2 * height * n + start, skip, dab, hid)

    each_half(part[0], height, half)


def weight_grads(part, rows, dab, hid, per_step=2):
    n_z, both, padded = rows.shape
    height = (padded - PAD) // (2 * BLOCKS)
    count, cols = dab.shape[0], dab.shape[1] + hid.shape[1]
    return pl.pallas_call(
        grads_kernel,
        grid_spec=pltpu.PrefetchScalarGridSpec(
            num_scalar_prefetch=1,
            grid=(BLOCKS // per_step,),
            in_specs=[
                pl.BlockSpec((n_z, both, 2 * height * per_step), lambda i, part: (0, 0, i)),
                pl.BlockSpec(dab.shape, lambda i, part: (0, 0)),
                pl.BlockSpec(hid.shape, lambda i, part: (0, 0)),
            ],
            out_specs=pl.BlockSpec((per_step, height, cols), lambda i, part: (i, 0, 0)),
        ),
        out_shape=jax.ShapeDtypeStruct((BLOCKS, height, cols), jnp.bfloat16),
        compiler_params=pltpu.CompilerParams(vmem_limit_bytes=VMEM_LIMIT),
        cost_estimate=pl.CostEstimate(
            flops=count * (padded - PAD) * cols, bytes_accessed=9_000_000, transcendentals=0
        ),
    )(jnp.reshape(part, (1,)).astype(jnp.int32), rows, dab, hid)


def other_kernel(place, keep_a, keep_b, got_a, got_b, acts, out_a, out_b, dab, hid):
    tok, hidden = got_a.shape[2] // 2, hid.shape[1] // 2
    count, cut, reach = dab.shape[0], keep_a.shape[1], got_a.shape[3]
    edge = 3 * hidden
    step = pl.program_id(0)

    @pl.when(step == 0)
    def _():
        rows = flat(acts[0])
        dab[:, :edge] = rows[:count]
        dab[:, edge:] = rows[count:, :hidden]
        hid[...] = rows[count:, hidden:]

    def dots(block, at, slices):
        columns = slice(at, at + 2 * hidden)
        pairs = pl.ds(pl.multiple_of(slices[0] * 2 * hidden, 128), slices[1] * 2 * hidden)
        ones = pl.ds(pl.multiple_of(slices[0] * hidden, 128), slices[1] * hidden)
        return dot_f32(block[:, :tok, columns], dab[:, pairs]), dot_f32(
            block[:, tok:, columns], hid[:, ones]
        )

    def put(start):
        from_x, from_g = dots(got_a[0], 0, (0, 2))
        rows = slice(start, start + cut)
        for i in range(2):
            col = 3 * i * hidden
            for at, part in (
                (col, from_x[rows, 2 * i * hidden : 2 * (i + 1) * hidden]),
                (col + 2 * hidden, from_g[rows, i * hidden : (i + 1) * hidden]),
            ):
                to = slice(at, at + part.shape[1])
                out_a[0, 0, :, to] = (keep_a[0, :, to].astype(jnp.float32) + part).astype(out_a.dtype)
        first = reach - 2 * hidden
        rows = slice(start + cut - first, start + 2 * cut - first)
        for m in range(2):
            from_x, from_g = dots(got_b[m], first, (place[8 + step], 1))
            for at, part in ((0, from_x[rows]), (2 * hidden, from_g[rows])):
                to = slice(at, at + part.shape[1])
                out_b[0, m, :, to] = (keep_b[m, :, to].astype(jnp.float32) + part).astype(out_b.dtype)

    @pl.when(place[12] == 0)
    def _():
        put(0)

    @pl.when(place[12] == 1)
    def _():
        put(reach - 2 * cut)


def core_sum(keep, got, slots):
    x, core, yh = lax.axis_index("x"), lax.axis_index("core"), lax.axis_index("yh")
    blocks, part, cols = keep.shape
    n_x, half, cut, width = blocks // 2, cols // 2, part // 2, blocks * part
    up = (x + core) % 2 == 0
    after, before = (x + 1) % 4, (x + 3) % 4
    a_slots = [x, jnp.where(up, after, before), jnp.where(up, before, after), (x + 2) % 4]
    far = jnp.where(core == 0, 1 - yh, yh)
    b_slots = [(yh, 0), (1 - far, 1), (far, 1), (1 - yh, 0)]
    place = [h * n_x + a_slots[s] for s in slots for h in range(2)]
    place += [h * 2 + m for h, _ in [b_slots[s] for s in slots] for m in range(2)]
    place += [c for _, c in [b_slots[s] for s in slots] for m in range(2)] + [core]
    place = jnp.stack([jnp.asarray(v, jnp.int32) for v in place])

    in_a = pl.BlockSpec((1, cut, cols), lambda j, p: (p[j], 0, 0))
    in_b = pl.BlockSpec((2, cut, half), lambda j, p: (p[4 + j], 1, p[8 + j]))

    def out(j, p):
        return (j // 2, j % 2, 0, 0)

    _, n_z, both, reach = got.shape
    count, hidden = n_z * both // 2, cols // 6
    return pl.pallas_call(
        other_kernel,
        grid_spec=pltpu.PrefetchScalarGridSpec(
            num_scalar_prefetch=1,
            grid=(4,),
            in_specs=[
                in_a,
                in_b,
                pl.BlockSpec((1, n_z, both, reach), lambda j, p: (p[j], 0, 0, 0)),
                pl.BlockSpec((2, n_z, both, reach), lambda j, p: (p[4 + j], 0, 0, 0)),
                pl.BlockSpec((1, n_z, both, reach), lambda j, p: (blocks, 0, 0, 0)),
            ],
            out_specs=[
                pl.BlockSpec((1, 1, cut, cols), out),
                pl.BlockSpec((1, 2, cut, half), out),
            ],
            scratch_shapes=[
                pltpu.VMEM((count, 4 * hidden), keep.dtype),
                pltpu.VMEM((count, 2 * hidden), keep.dtype),
            ],
        ),
        out_shape=[
            jax.ShapeDtypeStruct((2, 2, cut, cols), keep.dtype),
            jax.ShapeDtypeStruct((2, n_x, cut, half), keep.dtype),
        ],
        compiler_params=pltpu.CompilerParams(vmem_limit_bytes=VMEM_LIMIT),
        cost_estimate=pl.CostEstimate(
            flops=count * width * cols, bytes_accessed=9_000_000, transcendentals=0
        ),
    )(place, keep, keep, got, got, got)


def route_columns(expert_index, slot, gate):
    experts = jnp.arange(PAD, dtype=jnp.int32)
    hit = (expert_index[:, :, None] == experts) & (slot >= 0)[:, :, None]
    live = jnp.sum(hit.astype(jnp.float32), axis=1)
    weight = jnp.sum(jnp.where(hit, gate[:, :, None].astype(jnp.float32), 0.0), axis=1)
    return live.astype(jnp.bfloat16), weight.astype(jnp.bfloat16)


def add(*terms):
    return sum(t.astype(jnp.float32) for t in terms).astype(jnp.bfloat16)


def take(array, index, axis):
    return lax.dynamic_index_in_dim(array, index, axis, keepdims=False)


def pair_steps(place):
    return [
        [
            (place(p, c), place(p ^ 1 if (c + step) % 2 == 0 else 3 - p, c))
            for p in range(4)
            for c in range(2)
        ]
        for step in range(2)
    ]


X_RING = ("x", "core"), pair_steps(lambda p, c: p * 2 + c)
Y_RING = ("yh", "core", "yl"), pair_steps(lambda p, c: (p // 2 * 2 + c) * 2 + p % 2)


def pair_sum(ring, own, second, send):
    axes, (step1, step2) = ring
    got = lax.ppermute(send, axes, step1)
    last = lax.ppermute(add(second, got[1]), axes, step2)
    return add(own, got[0], last)


def x_blocks(blocks, axis):
    x, core = lax.axis_index("x"), lax.axis_index("core")
    up = (x + core) % 2 == 0
    after, before = (x + 1) % 4, (x + 3) % 4
    first, second = jnp.where(up, after, before), jnp.where(up, before, after)
    own, first, second, across = [take(blocks, at, axis) for at in (x, first, second, (x + 2) % 4)]
    return own, second, jnp.stack([first, across])


def y_blocks(blocks):
    yh, even = lax.axis_index("yh"), lax.axis_index("core") == 0
    cols = blocks.shape[-1] // 2
    here, there = take(blocks, yh, 0), take(blocks, 1 - yh, 0)
    near, far = here[..., cols:], there[..., cols:]
    first, second = jnp.where(even, near, far), jnp.where(even, far, near)
    return here[..., :cols], second, jnp.stack([first, there[..., :cols]])


def reduce_weights(swap, rows, dab, hid):
    core = lax.axis_index("core")
    got = lax.ppermute(swap, "core", SWAP)
    keep = weight_grads(core, rows, dab, hid)
    send_a, send_b = core_sum(keep, got, (1, 3))
    own_a, own_b = core_sum(keep, got, (0, 2))
    upper = pair_sum(X_RING, own_a[0], own_a[1], send_a)
    lower = pair_sum(Y_RING, own_b[0], own_b[1], send_b)
    upper = pair_sum(Y_RING, *y_blocks(upper))
    lower = pair_sum(X_RING, *x_blocks(lower, 0))
    return jnp.concatenate([upper, lower], axis=0)


def partner_weights(weights):
    core = lax.axis_index("core")
    half = take(weights.reshape(2, -1, weights.shape[1]), core, 0)
    mine = lax.ppermute(half, "yl", SWAP)
    other = lax.ppermute(mine, "core", SWAP)
    first = core == 0
    return jnp.concatenate([jnp.where(first, mine, other), jnp.where(first, other, mine)], axis=0)


def local(tokens, out_grad, expert_index, slot, gate, w_gate, w_up, w_down):
    tok, width = tokens.shape
    n_yl, n_z = lax.axis_size("yl"), lax.axis_size("z")
    hidden = w_gate.shape[2]
    yl, z = lax.axis_index("yl"), lax.axis_index("z")
    experts = [(row * n_z + z) // SPLIT for row in (yl, 1 - yl)]

    live, weight = route_columns(expert_index, slot, gate)
    send = jnp.concatenate(
        [
            jnp.concatenate([tokens, live], axis=1),
            jnp.concatenate([out_grad, weight], axis=1),
        ],
        axis=0,
    )
    rows = lax.all_gather(send, "z", axis=0, tiled=True)

    own = jnp.concatenate([w_gate[0], w_up[0], w_down[0]], axis=1)
    partner = partner_weights(own)
    pairs = 2 * hidden
    weights = jnp.concatenate(
        [own[:, :pairs], partner[:, :pairs], own[:, pairs:], partner[:, pairs:]], axis=1
    )

    rows = rows.reshape(n_z, 2 * tok, width + PAD)
    scalars = jnp.stack([*experts, 1 - lax.axis_index("core")]).astype(jnp.int32)
    back, dab, hid, swap = forward(scalars, rows, weights)
    grads = reduce_weights(swap, rows, dab, hid)
    input_grad = lax.psum_scatter(back, "z", scatter_dimension=0, tiled=True)
    return (
        input_grad,
        grads[None, :, :hidden],
        grads[None, :, hidden : 2 * hidden],
        grads[None, :, 2 * hidden :],
    )


def solution(mesh):
    fine = Mesh(mesh.devices.reshape(2, 4, 2, 2, 16), ("yh", "x", "core", "yl", "z"))
    every = P(("yh", "x", "core", "yl", "z"), None)
    slices = P(("yl", "z"), None, None)
    grads = P(("yl", "z"), ("yh", "x", "core"), None)
    return jax.shard_map(
        local,
        mesh=fine,
        in_specs=(every, every, every, every, every, slices, slices, slices),
        out_specs=(every, grads, grads, grads),
        check_vma=False,
    )
```

```python
import jax
import jax.numpy as jnp
from jax import lax
from jax.experimental import pallas as pl
from jax.experimental.pallas import tpu as pltpu
from jax.sharding import Mesh
from jax.sharding import PartitionSpec as P

WINDOW_EXPERTS = 4
SPLIT = 8
PAD = 128
CHUNKS = 10
BLOCKS = 8
VMEM_LIMIT = 60 * 1024 * 1024
VMEM_SMALL = 24 * 1024 * 1024
SWAP = [(0, 1), (1, 0)]


def flat(block):
    return block.reshape(-1, block.shape[-1])


def dot_f32(block, other):
    return lax.dot_general(
        flat(block), other, (((0,), (0,)), ((), ())), preferred_element_type=jnp.float32
    )


def dot_rows(block, other):
    return dot_f32(block, other).astype(jnp.bfloat16)


def put_grads(out, rows, at, skip, dab, hid):
    height, tok, hidden = out.shape[0], rows.shape[1] // 2, hid.shape[1] // 2
    reach = -(-height // 128) * 128
    columns = pl.ds(at, reach)
    from_x = dot_rows(rows[:, :tok, columns], dab[...])
    from_g = dot_rows(rows[:, tok:, columns], hid[...])
    fill_grads(out, from_x, from_g, skip, hidden)


def fill_grads(out, from_x, from_g, skip, hidden):
    height = out.shape[0]
    for i in range(2):
        col = 3 * i * hidden
        out[:, col : col + 2 * hidden] = from_x[
            skip : skip + height, 2 * i * hidden : 2 * (i + 1) * hidden
        ]
        out[:, col + 2 * hidden : col + 3 * hidden] = from_g[
            skip : skip + height, i * hidden : (i + 1) * hidden
        ]


def each_half(part, height, body):
    reach = -(-height // 128) * 128

    @pl.when(part == 0)
    def _():
        body(0, 0)

    @pl.when(part == 1)
    def _():
        body(2 * height - reach, reach - height)


def forward_kernel(
    scalars, rows, weights, back, dab, hid, swap, rows_v, w_v, back_v, acts_v, total, sems
):
    n_z, both, _ = rows_v.shape
    chunk = w_v.shape[1]
    tok = both // 2
    hidden = hid.shape[1] // 2
    width = CHUNKS * chunk
    blocks, reach = swap.shape[0] - 1, swap.shape[-1]
    step = width // blocks

    def columns(k):
        return pl.ds(pl.multiple_of(k * chunk, 128), chunk)

    def row_copy(k):
        at = columns(k)
        return pltpu.make_async_copy(rows.at[:, :, at], rows_v.at[:, :, at], sems.at[0, k])

    def weight_copy(k):
        return pltpu.make_async_copy(weights.at[columns(k), :], w_v.at[k], sems.at[1, k])

    def back_copy(k):
        return pltpu.make_async_copy(back_v.at[k], back.at[:, columns(k)], sems.at[2, k])

    def swap_copy(n):
        at = pl.ds(pl.multiple_of(n * step + scalars[2] * (step - reach), 128), reach)
        return pltpu.make_async_copy(rows_v.at[:, :, at], swap.at[n], sems.at[3, n])

    acts_copy = pltpu.make_async_copy(acts_v, swap.at[blocks], sems.at[3, blocks])
    last = pl.ds(width, PAD)
    route_copy = pltpu.make_async_copy(rows.at[:, :, last], rows_v.at[:, :, last], sems.at[4, 0])

    for k in range(CHUNKS):
        row_copy(k).start()
        weight_copy(k).start()
    route_copy.start()

    for k in range(CHUNKS):
        row_copy(k).wait()
        weight_copy(k).wait()
        at = slice(k * chunk, (k + 1) * chunk)
        x_rows, g_rows = flat(rows_v[:, :tok, at]), flat(rows_v[:, tok:, at])
        from_x = jnp.dot(x_rows, w_v[k, :, : 4 * hidden], preferred_element_type=jnp.float32)
        from_g = jnp.dot(g_rows, w_v[k, :, 4 * hidden :], preferred_element_type=jnp.float32)
        if k == 0:
            total[:, : 4 * hidden] = from_x
            total[:, 4 * hidden :] = from_g
        else:
            total[:, : 4 * hidden] += from_x
            total[:, 4 * hidden :] += from_g
    route_copy.wait()
    for n in range(blocks):
        swap_copy(n).start()

    live_rows = flat(rows_v[:, :tok, width:]).astype(jnp.float32)
    gate_rows = flat(rows_v[:, tok:, width:]).astype(jnp.float32)
    lanes = lax.broadcasted_iota(jnp.int32, live_rows.shape, 1)
    for i in range(2):
        mine = lanes == scalars[i]
        live = jnp.sum(jnp.where(mine, live_rows, 0.0), axis=1, keepdims=True) > 0
        gate = jnp.sum(jnp.where(mine, gate_rows, 0.0), axis=1, keepdims=True)
        at = 2 * i * hidden
        act_a = total[:, at : at + hidden]
        act_b = total[:, at + hidden : at + 2 * hidden]
        grad_h = total[:, (4 + i) * hidden : (5 + i) * hidden] * gate
        sig = 1.0 / (1.0 + jnp.exp(-act_a))
        silu = act_a * sig
        grad_a = grad_h * act_b * sig * (1.0 + act_a * (1.0 - sig))
        dab[:, at : at + hidden] = jnp.where(live, grad_a, 0.0).astype(dab.dtype)
        dab[:, at + hidden : at + 2 * hidden] = jnp.where(live, grad_h * silu, 0.0).astype(dab.dtype)
        hid[:, i * hidden : (i + 1) * hidden] = jnp.where(live, silu * act_b * gate, 0.0).astype(
            hid.dtype
        )

    edge = 3 * hidden
    acts = jnp.concatenate(
        [dab[:, :edge], jnp.concatenate([dab[:, edge:], hid[...]], axis=1)], axis=0
    )
    acts_v[...] = acts.reshape(acts_v.shape)
    acts_copy.start()

    for k in range(CHUNKS):
        back_v[k] = lax.dot_general(
            dab[...],
            w_v[k, :, : 4 * hidden],
            (((1,), (1,)), ((), ())),
            preferred_element_type=jnp.float32,
        ).astype(back_v.dtype)
        back_copy(k).start()

    for k in range(CHUNKS):
        back_copy(k).wait()
    for n in range(blocks):
        swap_copy(n).wait()
    acts_copy.wait()


def forward(scalars, rows, weights):
    n_z, both, padded = rows.shape
    width, cols = weights.shape
    hidden, chunk, count = cols // 6, width // CHUNKS, n_z * both // 2
    reach = -(-width // (2 * BLOCKS) // 128) * 128
    bf16 = jnp.bfloat16
    vmem = pl.BlockSpec(memory_space=pltpu.VMEM)
    hbm = pl.BlockSpec(memory_space=pl.ANY)
    return pl.pallas_call(
        forward_kernel,
        out_shape=(
            jax.ShapeDtypeStruct((count, width), bf16),
            jax.ShapeDtypeStruct((count, 4 * hidden), bf16),
            jax.ShapeDtypeStruct((count, 2 * hidden), bf16),
            jax.ShapeDtypeStruct((BLOCKS + 1, n_z, both, reach), bf16),
        ),
        in_specs=[pl.BlockSpec(memory_space=pltpu.SMEM), hbm, hbm],
        out_specs=(hbm, vmem, vmem, hbm),
        scratch_shapes=[
            pltpu.VMEM((n_z, both, padded), bf16),
            pltpu.VMEM((CHUNKS, chunk, cols), bf16),
            pltpu.VMEM((CHUNKS, count, chunk), bf16),
            pltpu.VMEM((n_z, both, reach), bf16),
            pltpu.VMEM((count, cols), jnp.float32),
            pltpu.SemaphoreType.DMA((5, CHUNKS + BLOCKS)),
        ],
        compiler_params=pltpu.CompilerParams(vmem_limit_bytes=VMEM_LIMIT),
        cost_estimate=pl.CostEstimate(
            flops=2 * count * width * 10 * hidden, bytes_accessed=20_000_000, transcendentals=0
        ),
    )(scalars, rows, weights)


def grads_kernel(part, rows, dab, hid, out):
    count, height, _ = out.shape

    def half(start, skip):
        for n in range(count):
            put_grads(out.at[n], rows, 2 * height * n + start, skip, dab, hid)

    each_half(part[0], height, half)


def weight_grads(part, rows, dab, hid, per_step=2):
    n_z, both, padded = rows.shape
    height = (padded - PAD) // (2 * BLOCKS)
    count, cols = dab.shape[0], dab.shape[1] + hid.shape[1]
    return pl.pallas_call(
        grads_kernel,
        grid_spec=pltpu.PrefetchScalarGridSpec(
            num_scalar_prefetch=1,
            grid=(BLOCKS // per_step,),
            in_specs=[
                pl.BlockSpec((n_z, both, 2 * height * per_step), lambda i, part: (0, 0, i)),
                pl.BlockSpec(dab.shape, lambda i, part: (0, 0)),
                pl.BlockSpec(hid.shape, lambda i, part: (0, 0)),
            ],
            out_specs=pl.BlockSpec((per_step, height, cols), lambda i, part: (i, 0, 0)),
        ),
        out_shape=jax.ShapeDtypeStruct((BLOCKS, height, cols), jnp.bfloat16),
        compiler_params=pltpu.CompilerParams(vmem_limit_bytes=VMEM_SMALL),
        cost_estimate=pl.CostEstimate(
            flops=count * (padded - PAD) * cols, bytes_accessed=9_000_000, transcendentals=0
        ),
    )(jnp.reshape(part, (1,)).astype(jnp.int32), rows, dab, hid)


def other_kernel(place, keep_a, keep_b, got_a, got_b, acts, out_a, out_b, dab, hid):
    tok, hidden = got_a.shape[2] // 2, hid.shape[1] // 2
    count, cut, reach = dab.shape[0], keep_a.shape[1], got_a.shape[3]
    edge = 3 * hidden
    step = pl.program_id(0)

    @pl.when(step == 0)
    def _():
        rows = flat(acts[0])
        dab[:, :edge] = rows[:count]
        dab[:, edge:] = rows[count:, :hidden]
        hid[...] = rows[count:, hidden:]

    def dots(block, at, slices):
        columns = slice(at, at + 2 * hidden)
        pairs = pl.ds(pl.multiple_of(slices[0] * 2 * hidden, 128), slices[1] * 2 * hidden)
        ones = pl.ds(pl.multiple_of(slices[0] * hidden, 128), slices[1] * hidden)
        return dot_f32(block[:, :tok, columns], dab[:, pairs]), dot_f32(
            block[:, tok:, columns], hid[:, ones]
        )

    def put(start):
        from_x, from_g = dots(got_a[0], 0, (0, 2))
        rows = slice(start, start + cut)
        for i in range(2):
            col = 3 * i * hidden
            for at, part in (
                (col, from_x[rows, 2 * i * hidden : 2 * (i + 1) * hidden]),
                (col + 2 * hidden, from_g[rows, i * hidden : (i + 1) * hidden]),
            ):
                to = slice(at, at + part.shape[1])
                out_a[0, 0, :, to] = (keep_a[0, :, to].astype(jnp.float32) + part).astype(out_a.dtype)
        first = reach - 2 * hidden
        rows = slice(start + cut - first, start + 2 * cut - first)
        for m in range(2):
            from_x, from_g = dots(got_b[m], first, (place[8 + step], 1))
            for at, part in ((0, from_x[rows]), (2 * hidden, from_g[rows])):
                to = slice(at, at + part.shape[1])
                out_b[0, m, :, to] = (keep_b[m, :, to].astype(jnp.float32) + part).astype(out_b.dtype)

    @pl.when(place[12] == 0)
    def _():
        put(0)

    @pl.when(place[12] == 1)
    def _():
        put(reach - 2 * cut)


def core_sum(keep, got, slots):
    x, core, yh = lax.axis_index("x"), lax.axis_index("core"), lax.axis_index("yh")
    blocks, part, cols = keep.shape
    n_x, half, cut, width = blocks // 2, cols // 2, part // 2, blocks * part
    up = (x + core) % 2 == 0
    after, before = (x + 1) % 4, (x + 3) % 4
    a_slots = [x, jnp.where(up, after, before), jnp.where(up, before, after), (x + 2) % 4]
    far = jnp.where(core == 0, 1 - yh, yh)
    b_slots = [(yh, 0), (1 - far, 1), (far, 1), (1 - yh, 0)]
    place = [h * n_x + a_slots[s] for s in slots for h in range(2)]
    place += [h * 2 + m for h, _ in [b_slots[s] for s in slots] for m in range(2)]
    place += [c for _, c in [b_slots[s] for s in slots] for m in range(2)] + [core]
    place = jnp.stack([jnp.asarray(v, jnp.int32) for v in place])

    in_a = pl.BlockSpec((1, cut, cols), lambda j, p: (p[j], 0, 0))
    in_b = pl.BlockSpec((2, cut, half), lambda j, p: (p[4 + j], 1, p[8 + j]))

    def out(j, p):
        return (j // 2, j % 2, 0, 0)

    _, n_z, both, reach = got.shape
    count, hidden = n_z * both // 2, cols // 6
    return pl.pallas_call(
        other_kernel,
        grid_spec=pltpu.PrefetchScalarGridSpec(
            num_scalar_prefetch=1,
            grid=(4,),
            in_specs=[
                in_a,
                in_b,
                pl.BlockSpec((1, n_z, both, reach), lambda j, p: (p[j], 0, 0, 0)),
                pl.BlockSpec((2, n_z, both, reach), lambda j, p: (p[4 + j], 0, 0, 0)),
                pl.BlockSpec((1, n_z, both, reach), lambda j, p: (blocks, 0, 0, 0)),
            ],
            out_specs=[
                pl.BlockSpec((1, 1, cut, cols), out),
                pl.BlockSpec((1, 2, cut, half), out),
            ],
            scratch_shapes=[
                pltpu.VMEM((count, 4 * hidden), keep.dtype),
                pltpu.VMEM((count, 2 * hidden), keep.dtype),
            ],
        ),
        out_shape=[
            jax.ShapeDtypeStruct((2, 2, cut, cols), keep.dtype),
            jax.ShapeDtypeStruct((2, n_x, cut, half), keep.dtype),
        ],
        compiler_params=pltpu.CompilerParams(vmem_limit_bytes=VMEM_SMALL),
        cost_estimate=pl.CostEstimate(
            flops=count * width * cols, bytes_accessed=9_000_000, transcendentals=0
        ),
    )(place, keep, keep, got, got, got)


def pack_kernel(expert_index, slot, gate, tokens, out_grad, out):
    tok, width = tokens.shape
    out[:tok, :width] = tokens[...]
    out[tok:, :width] = out_grad[...]
    square = (tok, tok)
    eye = lax.broadcasted_iota(jnp.int32, square, 0) == lax.broadcasted_iota(jnp.int32, square, 1)

    def column(row):
        spread = jnp.broadcast_to(row.astype(jnp.float32), square)
        return jnp.sum(jnp.where(eye, spread, 0.0), axis=1, keepdims=True)

    lanes = lax.broadcasted_iota(jnp.int32, (tok, PAD), 1).astype(jnp.float32)
    live, weight = jnp.zeros((tok, PAD), jnp.float32), jnp.zeros((tok, PAD), jnp.float32)
    gates = gate[...].astype(jnp.float32)
    for r in range(expert_index.shape[0]):
        row = slice(r, r + 1)
        hit = (lanes == column(expert_index[row])) & (column(slot[row]) >= 0)
        live += jnp.where(hit, 1.0, 0.0)
        weight += jnp.where(hit, column(gates[row]), 0.0)
    out[:tok, width:] = live.astype(out.dtype)
    out[tok:, width:] = weight.astype(out.dtype)


def pack(tokens, out_grad, expert_index, slot, gate):
    tok, width = tokens.shape
    vmem = pl.BlockSpec(memory_space=pltpu.VMEM)
    return pl.pallas_call(
        pack_kernel,
        out_shape=jax.ShapeDtypeStruct((2 * tok, width + PAD), tokens.dtype),
        in_specs=[vmem] * 5,
        out_specs=vmem,
        compiler_params=pltpu.CompilerParams(vmem_limit_bytes=VMEM_LIMIT),
        cost_estimate=pl.CostEstimate(flops=0, bytes_accessed=700_000, transcendentals=0),
    )(expert_index.T, slot.T, gate.T, tokens, out_grad)


def add(*terms):
    return sum(t.astype(jnp.float32) for t in terms).astype(jnp.bfloat16)


def take(array, index, axis):
    return lax.dynamic_index_in_dim(array, index, axis, keepdims=False)


def pair_steps(place):
    return [
        [
            (place(p, c), place(p ^ 1 if (c + step) % 2 == 0 else 3 - p, c))
            for p in range(4)
            for c in range(2)
        ]
        for step in range(2)
    ]


X_RING = ("x", "core"), pair_steps(lambda p, c: p * 2 + c)
Y_RING = ("yh", "core", "yl"), pair_steps(lambda p, c: (p // 2 * 2 + c) * 2 + p % 2)


def pair_sum(ring, own, second, send):
    axes, (step1, step2) = ring
    got = lax.ppermute(send, axes, step1)
    last = lax.ppermute(add(second, got[1]), axes, step2)
    return add(own, got[0], last)


def x_blocks(blocks, axis):
    x, core = lax.axis_index("x"), lax.axis_index("core")
    up = (x + core) % 2 == 0
    after, before = (x + 1) % 4, (x + 3) % 4
    first, second = jnp.where(up, after, before), jnp.where(up, before, after)
    own, first, second, across = [take(blocks, at, axis) for at in (x, first, second, (x + 2) % 4)]
    return own, second, jnp.stack([first, across])


def y_blocks(blocks):
    yh, even = lax.axis_index("yh"), lax.axis_index("core") == 0
    cols = blocks.shape[-1] // 2
    here, there = take(blocks, yh, 0), take(blocks, 1 - yh, 0)
    near, far = here[..., cols:], there[..., cols:]
    first, second = jnp.where(even, near, far), jnp.where(even, far, near)
    return here[..., :cols], second, jnp.stack([first, there[..., :cols]])


def reduce_weights(swap, rows, dab, hid):
    core = lax.axis_index("core")
    got = lax.ppermute(swap, "core", SWAP)
    keep = weight_grads(core, rows, dab, hid)
    send_a, send_b = core_sum(keep, got, (1, 3))
    own_a, own_b = core_sum(keep, got, (0, 2))
    upper = pair_sum(X_RING, own_a[0], own_a[1], send_a)
    lower = pair_sum(Y_RING, own_b[0], own_b[1], send_b)
    upper = pair_sum(Y_RING, *y_blocks(upper))
    lower = pair_sum(X_RING, *x_blocks(lower, 0))
    return jnp.concatenate([upper, lower], axis=0)


def partner_weights(weights):
    core = lax.axis_index("core")
    half = take(weights.reshape(2, -1, weights.shape[1]), core, 0)
    mine = lax.ppermute(half, "yl", SWAP)
    other = lax.ppermute(mine, "core", SWAP)
    first = core == 0
    return jnp.concatenate([jnp.where(first, mine, other), jnp.where(first, other, mine)], axis=0)


def local(tokens, out_grad, expert_index, slot, gate, w_gate, w_up, w_down):
    tok, width = tokens.shape
    n_yl, n_z = lax.axis_size("yl"), lax.axis_size("z")
    hidden = w_gate.shape[2]
    yl, z = lax.axis_index("yl"), lax.axis_index("z")
    experts = [(row * n_z + z) // SPLIT for row in (yl, 1 - yl)]

    send = pack(tokens, out_grad, expert_index, slot, gate)
    rows = lax.all_gather(send, "z", axis=0, tiled=True)

    own = jnp.concatenate([w_gate[0], w_up[0], w_down[0]], axis=1)
    partner = partner_weights(own)
    pairs = 2 * hidden
    weights = jnp.concatenate(
        [own[:, :pairs], partner[:, :pairs], own[:, pairs:], partner[:, pairs:]], axis=1
    )

    rows = rows.reshape(n_z, 2 * tok, width + PAD)
    scalars = jnp.stack([*experts, 1 - lax.axis_index("core")]).astype(jnp.int32)
    back, dab, hid, swap = forward(scalars, rows, weights)
    grads = reduce_weights(swap, rows, dab, hid)
    input_grad = lax.psum_scatter(back, "z", scatter_dimension=0, tiled=True)
    return (
        input_grad,
        grads[None, :, :hidden],
        grads[None, :, hidden : 2 * hidden],
        grads[None, :, 2 * hidden :],
    )


def solution(mesh):
    fine = Mesh(mesh.devices.reshape(2, 4, 2, 2, 16), ("yh", "x", "core", "yl", "z"))
    every = P(("yh", "x", "core", "yl", "z"), None)
    slices = P(("yl", "z"), None, None)
    grads = P(("yl", "z"), ("yh", "x", "core"), None)
    return jax.shard_map(
        local,
        mesh=fine,
        in_specs=(every, every, every, every, every, slices, slices, slices),
        out_specs=(every, grads, grads, grads),
        check_vma=False,
    )
```

```python
import jax
import jax.numpy as jnp
from jax import lax
from jax.experimental import pallas as pl
from jax.experimental.pallas import tpu as pltpu
from jax.sharding import Mesh
from jax.sharding import PartitionSpec as P

WINDOW_EXPERTS = 4
SPLIT = 8
PAD = 128
CHUNKS = 10
BLOCKS = 8
VMEM_LIMIT = 60 * 1024 * 1024
VMEM_SMALL = 24 * 1024 * 1024
SWAP = [(0, 1), (1, 0)]


def flat(block):
    return block.reshape(-1, block.shape[-1])


def dot_f32(block, other):
    return lax.dot_general(
        flat(block), other, (((0,), (0,)), ((), ())), preferred_element_type=jnp.float32
    )


def dot_rows(block, other):
    return dot_f32(block, other).astype(jnp.bfloat16)


def put_grads(out, rows, at, skip, dab, hid):
    height, tok, hidden = out.shape[0], rows.shape[1] // 2, hid.shape[1] // 2
    reach = -(-height // 128) * 128
    columns = pl.ds(at, reach)
    from_x = dot_rows(rows[:, :tok, columns], dab[...])
    from_g = dot_rows(rows[:, tok:, columns], hid[...])
    fill_grads(out, from_x, from_g, skip, hidden)


def fill_grads(out, from_x, from_g, skip, hidden):
    height = out.shape[0]
    for i in range(2):
        col = 3 * i * hidden
        out[:, col : col + 2 * hidden] = from_x[
            skip : skip + height, 2 * i * hidden : 2 * (i + 1) * hidden
        ]
        out[:, col + 2 * hidden : col + 3 * hidden] = from_g[
            skip : skip + height, i * hidden : (i + 1) * hidden
        ]


def each_half(part, height, body):
    reach = -(-height // 128) * 128

    @pl.when(part == 0)
    def _():
        body(0, 0)

    @pl.when(part == 1)
    def _():
        body(2 * height - reach, reach - height)


def forward_kernel(
    scalars, rows, weights, back, dab, hid, swap, rows_v, w_v, back_v, acts_v, total, sems
):
    n_z, both, _ = rows_v.shape
    chunk = w_v.shape[1]
    tok = both // 2
    hidden = hid.shape[1] // 2
    width = CHUNKS * chunk
    blocks, reach = swap.shape[0] - 1, swap.shape[-1]
    step = width // blocks

    def columns(k):
        return pl.ds(pl.multiple_of(k * chunk, 128), chunk)

    def row_copy(k):
        half, at = divmod(k * chunk, width // 2)
        source = rows.at[:, half * both : (half + 1) * both, at : at + chunk]
        return pltpu.make_async_copy(source, rows_v.at[:, :, columns(k)], sems.at[0, k])

    def weight_copy(k):
        return pltpu.make_async_copy(weights.at[columns(k), :], w_v.at[k], sems.at[1, k])

    def back_copy(k):
        return pltpu.make_async_copy(back_v.at[k], back.at[:, columns(k)], sems.at[2, k])

    def swap_copy(n):
        at = pl.ds(pl.multiple_of(n * step + scalars[2] * (step - reach), 128), reach)
        return pltpu.make_async_copy(rows_v.at[:, :, at], swap.at[n], sems.at[3, n])

    acts_copy = pltpu.make_async_copy(acts_v, swap.at[blocks], sems.at[3, blocks])
    route_copy = pltpu.make_async_copy(
        rows.at[:, :both, width // 2 :], rows_v.at[:, :, width:], sems.at[4, 0]
    )

    for k in range(CHUNKS):
        row_copy(k).start()
        weight_copy(k).start()
    route_copy.start()

    for k in range(CHUNKS):
        row_copy(k).wait()
        weight_copy(k).wait()
        at = slice(k * chunk, (k + 1) * chunk)
        x_rows, g_rows = flat(rows_v[:, :tok, at]), flat(rows_v[:, tok:, at])
        from_x = jnp.dot(x_rows, w_v[k, :, : 4 * hidden], preferred_element_type=jnp.float32)
        from_g = jnp.dot(g_rows, w_v[k, :, 4 * hidden :], preferred_element_type=jnp.float32)
        if k == 0:
            total[:, : 4 * hidden] = from_x
            total[:, 4 * hidden :] = from_g
        else:
            total[:, : 4 * hidden] += from_x
            total[:, 4 * hidden :] += from_g
    route_copy.wait()
    for n in range(blocks):
        swap_copy(n).start()

    live_rows = flat(rows_v[:, :tok, width:]).astype(jnp.float32)
    gate_rows = flat(rows_v[:, tok:, width:]).astype(jnp.float32)
    lanes = lax.broadcasted_iota(jnp.int32, live_rows.shape, 1)
    for i in range(2):
        mine = lanes == scalars[i]
        live = jnp.sum(jnp.where(mine, live_rows, 0.0), axis=1, keepdims=True) > 0
        gate = jnp.sum(jnp.where(mine, gate_rows, 0.0), axis=1, keepdims=True)
        at = 2 * i * hidden
        act_a = total[:, at : at + hidden]
        act_b = total[:, at + hidden : at + 2 * hidden]
        grad_h = total[:, (4 + i) * hidden : (5 + i) * hidden] * gate
        sig = 1.0 / (1.0 + jnp.exp(-act_a))
        silu = act_a * sig
        grad_a = grad_h * act_b * sig * (1.0 + act_a * (1.0 - sig))
        dab[:, at : at + hidden] = jnp.where(live, grad_a, 0.0).astype(dab.dtype)
        dab[:, at + hidden : at + 2 * hidden] = jnp.where(live, grad_h * silu, 0.0).astype(dab.dtype)
        hid[:, i * hidden : (i + 1) * hidden] = jnp.where(live, silu * act_b * gate, 0.0).astype(
            hid.dtype
        )

    edge = 3 * hidden
    acts = jnp.concatenate(
        [dab[:, :edge], jnp.concatenate([dab[:, edge:], hid[...]], axis=1)], axis=0
    )
    acts_v[...] = acts.reshape(acts_v.shape)
    acts_copy.start()

    for k in range(CHUNKS):
        back_v[k] = lax.dot_general(
            dab[...],
            w_v[k, :, : 4 * hidden],
            (((1,), (1,)), ((), ())),
            preferred_element_type=jnp.float32,
        ).astype(back_v.dtype)
        back_copy(k).start()

    for k in range(CHUNKS):
        back_copy(k).wait()
    for n in range(blocks):
        swap_copy(n).wait()
    acts_copy.wait()


def forward(scalars, rows, weights):
    n_z, both = rows.shape[0], rows.shape[1] // 2
    width, cols = weights.shape
    hidden, chunk, count = cols // 6, width // CHUNKS, n_z * both // 2
    reach = -(-width // (2 * BLOCKS) // 128) * 128
    bf16 = jnp.bfloat16
    vmem = pl.BlockSpec(memory_space=pltpu.VMEM)
    hbm = pl.BlockSpec(memory_space=pl.ANY)
    return pl.pallas_call(
        forward_kernel,
        out_shape=(
            jax.ShapeDtypeStruct((count, width), bf16),
            jax.ShapeDtypeStruct((count, 4 * hidden), bf16),
            jax.ShapeDtypeStruct((count, 2 * hidden), bf16),
            jax.ShapeDtypeStruct((BLOCKS + 1, n_z, both, reach), bf16),
        ),
        in_specs=[pl.BlockSpec(memory_space=pltpu.SMEM), hbm, hbm],
        out_specs=(hbm, vmem, vmem, hbm),
        scratch_shapes=[
            pltpu.VMEM((n_z, both, width + PAD), bf16),
            pltpu.VMEM((CHUNKS, chunk, cols), bf16),
            pltpu.VMEM((CHUNKS, count, chunk), bf16),
            pltpu.VMEM((n_z, both, reach), bf16),
            pltpu.VMEM((count, cols), jnp.float32),
            pltpu.SemaphoreType.DMA((5, CHUNKS + BLOCKS)),
        ],
        compiler_params=pltpu.CompilerParams(vmem_limit_bytes=VMEM_LIMIT),
        cost_estimate=pl.CostEstimate(
            flops=2 * count * width * 10 * hidden, bytes_accessed=20_000_000, transcendentals=0
        ),
    )(scalars, rows, weights)


def grads_kernel(part, rows, dab, hid, out):
    count, height, _ = out.shape

    def half(start, skip):
        for n in range(count):
            put_grads(out.at[n], rows, 2 * height * n + start, skip, dab, hid)

    each_half(part[0], height, half)


def weight_grads(part, rows, dab, hid, per_step=2):
    n_z, both = rows.shape[0], rows.shape[1] // 2
    width = 2 * (rows.shape[2] - PAD)
    height, steps = width // (2 * BLOCKS), BLOCKS // per_step
    count, cols = dab.shape[0], dab.shape[1] + hid.shape[1]
    return pl.pallas_call(
        grads_kernel,
        grid_spec=pltpu.PrefetchScalarGridSpec(
            num_scalar_prefetch=1,
            grid=(steps,),
            in_specs=[
                pl.BlockSpec(
                    (n_z, both, 2 * height * per_step),
                    lambda i, part: (0, i // (steps // 2), i % (steps // 2)),
                ),
                pl.BlockSpec(dab.shape, lambda i, part: (0, 0)),
                pl.BlockSpec(hid.shape, lambda i, part: (0, 0)),
            ],
            out_specs=pl.BlockSpec((per_step, height, cols), lambda i, part: (i, 0, 0)),
        ),
        out_shape=jax.ShapeDtypeStruct((BLOCKS, height, cols), jnp.bfloat16),
        compiler_params=pltpu.CompilerParams(vmem_limit_bytes=VMEM_SMALL),
        cost_estimate=pl.CostEstimate(
            flops=count * width * cols, bytes_accessed=9_000_000, transcendentals=0
        ),
    )(jnp.reshape(part, (1,)).astype(jnp.int32), rows, dab, hid)


def other_kernel(place, keep_a, keep_b, got_a, got_b, acts, out_a, out_b, dab, hid):
    tok, hidden = got_a.shape[2] // 2, hid.shape[1] // 2
    count, cut, reach = dab.shape[0], keep_a.shape[1], got_a.shape[3]
    edge = 3 * hidden
    step = pl.program_id(0)

    @pl.when(step == 0)
    def _():
        rows = flat(acts[0])
        dab[:, :edge] = rows[:count]
        dab[:, edge:] = rows[count:, :hidden]
        hid[...] = rows[count:, hidden:]

    def dots(block, at, slices):
        columns = slice(at, at + 2 * hidden)
        pairs = pl.ds(pl.multiple_of(slices[0] * 2 * hidden, 128), slices[1] * 2 * hidden)
        ones = pl.ds(pl.multiple_of(slices[0] * hidden, 128), slices[1] * hidden)
        return dot_f32(block[:, :tok, columns], dab[:, pairs]), dot_f32(
            block[:, tok:, columns], hid[:, ones]
        )

    def put(start):
        from_x, from_g = dots(got_a[0], 0, (0, 2))
        rows = slice(start, start + cut)
        for i in range(2):
            col = 3 * i * hidden
            for at, part in (
                (col, from_x[rows, 2 * i * hidden : 2 * (i + 1) * hidden]),
                (col + 2 * hidden, from_g[rows, i * hidden : (i + 1) * hidden]),
            ):
                to = slice(at, at + part.shape[1])
                out_a[0, 0, :, to] = (keep_a[0, :, to].astype(jnp.float32) + part).astype(out_a.dtype)
        first = reach - 2 * hidden
        rows = slice(start + cut - first, start + 2 * cut - first)
        for m in range(2):
            from_x, from_g = dots(got_b[m], first, (place[8 + step], 1))
            for at, part in ((0, from_x[rows]), (2 * hidden, from_g[rows])):
                to = slice(at, at + part.shape[1])
                out_b[0, m, :, to] = (keep_b[m, :, to].astype(jnp.float32) + part).astype(out_b.dtype)

    @pl.when(place[12] == 0)
    def _():
        put(0)

    @pl.when(place[12] == 1)
    def _():
        put(reach - 2 * cut)


def core_sum(keep, got, slots):
    x, core, yh = lax.axis_index("x"), lax.axis_index("core"), lax.axis_index("yh")
    blocks, part, cols = keep.shape
    n_x, half, cut, width = blocks // 2, cols // 2, part // 2, blocks * part
    up = (x + core) % 2 == 0
    after, before = (x + 1) % 4, (x + 3) % 4
    a_slots = [x, jnp.where(up, after, before), jnp.where(up, before, after), (x + 2) % 4]
    far = jnp.where(core == 0, 1 - yh, yh)
    b_slots = [(yh, 0), (1 - far, 1), (far, 1), (1 - yh, 0)]
    place = [h * n_x + a_slots[s] for s in slots for h in range(2)]
    place += [h * 2 + m for h, _ in [b_slots[s] for s in slots] for m in range(2)]
    place += [c for _, c in [b_slots[s] for s in slots] for m in range(2)] + [core]
    place = jnp.stack([jnp.asarray(v, jnp.int32) for v in place])

    in_a = pl.BlockSpec((1, cut, cols), lambda j, p: (p[j], 0, 0))
    in_b = pl.BlockSpec((2, cut, half), lambda j, p: (p[4 + j], 1, p[8 + j]))

    def out(j, p):
        return (j // 2, j % 2, 0, 0)

    _, n_z, both, reach = got.shape
    count, hidden = n_z * both // 2, cols // 6
    return pl.pallas_call(
        other_kernel,
        grid_spec=pltpu.PrefetchScalarGridSpec(
            num_scalar_prefetch=1,
            grid=(4,),
            in_specs=[
                in_a,
                in_b,
                pl.BlockSpec((1, n_z, both, reach), lambda j, p: (p[j], 0, 0, 0)),
                pl.BlockSpec((2, n_z, both, reach), lambda j, p: (p[4 + j], 0, 0, 0)),
                pl.BlockSpec((1, n_z, both, reach), lambda j, p: (blocks, 0, 0, 0)),
            ],
            out_specs=[
                pl.BlockSpec((1, 1, cut, cols), out),
                pl.BlockSpec((1, 2, cut, half), out),
            ],
            scratch_shapes=[
                pltpu.VMEM((count, 4 * hidden), keep.dtype),
                pltpu.VMEM((count, 2 * hidden), keep.dtype),
            ],
        ),
        out_shape=[
            jax.ShapeDtypeStruct((2, 2, cut, cols), keep.dtype),
            jax.ShapeDtypeStruct((2, n_x, cut, half), keep.dtype),
        ],
        compiler_params=pltpu.CompilerParams(vmem_limit_bytes=VMEM_SMALL),
        cost_estimate=pl.CostEstimate(
            flops=count * width * cols, bytes_accessed=9_000_000, transcendentals=0
        ),
    )(place, keep, keep, got, got, got)


def pack_kernel(expert_index, slot, gate, tokens, out_grad, out):
    tok, width = tokens.shape
    half = width // 2
    for i in range(2):
        columns = slice(i * half, (i + 1) * half)
        out[2 * i * tok : (2 * i + 1) * tok, :half] = tokens[:, columns]
        out[(2 * i + 1) * tok : 2 * (i + 1) * tok, :half] = out_grad[:, columns]
    square = (tok, tok)
    eye = lax.broadcasted_iota(jnp.int32, square, 0) == lax.broadcasted_iota(jnp.int32, square, 1)

    def column(row):
        spread = jnp.broadcast_to(row.astype(jnp.float32), square)
        return jnp.sum(jnp.where(eye, spread, 0.0), axis=1, keepdims=True)

    lanes = lax.broadcasted_iota(jnp.int32, (tok, PAD), 1).astype(jnp.float32)
    live, weight = jnp.zeros((tok, PAD), jnp.float32), jnp.zeros((tok, PAD), jnp.float32)
    gates = gate[...].astype(jnp.float32)
    for r in range(expert_index.shape[0]):
        row = slice(r, r + 1)
        hit = (lanes == column(expert_index[row])) & (column(slot[row]) >= 0)
        live += jnp.where(hit, 1.0, 0.0)
        weight += jnp.where(hit, column(gates[row]), 0.0)
    out[:tok, half:] = live.astype(out.dtype)
    out[tok : 2 * tok, half:] = weight.astype(out.dtype)
    out[2 * tok :, half:] = jnp.zeros((2 * tok, PAD), out.dtype)


def pack(tokens, out_grad, expert_index, slot, gate):
    tok, width = tokens.shape
    vmem = pl.BlockSpec(memory_space=pltpu.VMEM)
    return pl.pallas_call(
        pack_kernel,
        out_shape=jax.ShapeDtypeStruct((4 * tok, width // 2 + PAD), tokens.dtype),
        in_specs=[vmem] * 5,
        out_specs=vmem,
        compiler_params=pltpu.CompilerParams(vmem_limit_bytes=VMEM_LIMIT),
        cost_estimate=pl.CostEstimate(flops=0, bytes_accessed=700_000, transcendentals=0),
    )(expert_index.T, slot.T, gate.T, tokens, out_grad)


def add(*terms):
    return sum(t.astype(jnp.float32) for t in terms).astype(jnp.bfloat16)


def take(array, index, axis):
    return lax.dynamic_index_in_dim(array, index, axis, keepdims=False)


def pair_steps(place):
    return [
        [
            (place(p, c), place(p ^ 1 if (c + step) % 2 == 0 else 3 - p, c))
            for p in range(4)
            for c in range(2)
        ]
        for step in range(2)
    ]


X_RING = ("x", "core"), pair_steps(lambda p, c: p * 2 + c)
Y_RING = ("yh", "core", "yl"), pair_steps(lambda p, c: (p // 2 * 2 + c) * 2 + p % 2)


def pair_sum(ring, own, second, send):
    axes, (step1, step2) = ring
    got = lax.ppermute(send, axes, step1)
    last = lax.ppermute(add(second, got[1]), axes, step2)
    return add(own, got[0], last)


def x_blocks(blocks, axis):
    x, core = lax.axis_index("x"), lax.axis_index("core")
    up = (x + core) % 2 == 0
    after, before = (x + 1) % 4, (x + 3) % 4
    first, second = jnp.where(up, after, before), jnp.where(up, before, after)
    own, first, second, across = [take(blocks, at, axis) for at in (x, first, second, (x + 2) % 4)]
    return own, second, jnp.stack([first, across])


def y_blocks(blocks):
    yh, even = lax.axis_index("yh"), lax.axis_index("core") == 0
    cols = blocks.shape[-1] // 2
    here, there = take(blocks, yh, 0), take(blocks, 1 - yh, 0)
    near, far = here[..., cols:], there[..., cols:]
    first, second = jnp.where(even, near, far), jnp.where(even, far, near)
    return here[..., :cols], second, jnp.stack([first, there[..., :cols]])


def reduce_weights(swap, rows, dab, hid):
    core = lax.axis_index("core")
    got = lax.ppermute(swap, "core", SWAP)
    keep = weight_grads(core, rows, dab, hid)
    send_a, send_b = core_sum(keep, got, (1, 3))
    own_a, own_b = core_sum(keep, got, (0, 2))
    upper = pair_sum(X_RING, own_a[0], own_a[1], send_a)
    lower = pair_sum(Y_RING, own_b[0], own_b[1], send_b)
    upper = pair_sum(Y_RING, *y_blocks(upper))
    lower = pair_sum(X_RING, *x_blocks(lower, 0))
    return jnp.concatenate([upper, lower], axis=0)


def partner_weights(weights):
    core = lax.axis_index("core")
    half = take(weights.reshape(2, -1, weights.shape[1]), core, 0)
    mine = lax.ppermute(half, "yl", SWAP)
    other = lax.ppermute(mine, "core", SWAP)
    first = core == 0
    return jnp.concatenate([jnp.where(first, mine, other), jnp.where(first, other, mine)], axis=0)


def local(tokens, out_grad, expert_index, slot, gate, w_gate, w_up, w_down):
    tok, width = tokens.shape
    n_yl, n_z = lax.axis_size("yl"), lax.axis_size("z")
    hidden = w_gate.shape[2]
    yl, z = lax.axis_index("yl"), lax.axis_index("z")
    experts = [(row * n_z + z) // SPLIT for row in (yl, 1 - yl)]

    send = pack(tokens, out_grad, expert_index, slot, gate)
    rows = lax.all_gather(send, "z", axis=0, tiled=True)

    own = jnp.concatenate([w_gate[0], w_up[0], w_down[0]], axis=1)
    partner = partner_weights(own)
    pairs = 2 * hidden
    weights = jnp.concatenate(
        [own[:, :pairs], partner[:, :pairs], own[:, pairs:], partner[:, pairs:]], axis=1
    )

    rows = rows.reshape(n_z, 4 * tok, -1)
    scalars = jnp.stack([*experts, 1 - lax.axis_index("core")]).astype(jnp.int32)
    back, dab, hid, swap = forward(scalars, rows, weights)
    grads = reduce_weights(swap, rows, dab, hid)
    input_grad = lax.psum_scatter(back, "z", scatter_dimension=0, tiled=True)
    return (
        input_grad,
        grads[None, :, :hidden],
        grads[None, :, hidden : 2 * hidden],
        grads[None, :, 2 * hidden :],
    )


def solution(mesh):
    fine = Mesh(mesh.devices.reshape(2, 4, 2, 2, 16), ("yh", "x", "core", "yl", "z"))
    every = P(("yh", "x", "core", "yl", "z"), None)
    slices = P(("yl", "z"), None, None)
    grads = P(("yl", "z"), ("yh", "x", "core"), None)
    return jax.shard_map(
        local,
        mesh=fine,
        in_specs=(every, every, every, every, every, slices, slices, slices),
        out_specs=(every, grads, grads, grads),
        check_vma=False,
    )
```

```python
import jax
import jax.numpy as jnp
from jax import lax
from jax.experimental import pallas as pl
from jax.experimental.pallas import tpu as pltpu
from jax.sharding import Mesh
from jax.sharding import PartitionSpec as P

WINDOW_EXPERTS = 4
SPLIT = 8
PAD = 128
CHUNKS = 10
BLOCKS = 8
VMEM_LIMIT = 60 * 1024 * 1024
VMEM_SMALL = 24 * 1024 * 1024
SWAP = [(0, 1), (1, 0)]


def flat(block):
    return block.reshape(-1, block.shape[-1])


def dot_f32(block, other):
    return lax.dot_general(
        flat(block), other, (((0,), (0,)), ((), ())), preferred_element_type=jnp.float32
    )


def dot_rows(block, other):
    return dot_f32(block, other).astype(jnp.bfloat16)


def put_grads(out, rows, at, skip, dab, hid):
    height, tok, hidden = out.shape[0], rows.shape[1] // 2, hid.shape[1] // 2
    reach = -(-height // 128) * 128
    columns = pl.ds(at, reach)
    from_x = dot_rows(rows[:, :tok, columns], dab[...])
    from_g = dot_rows(rows[:, tok:, columns], hid[...])
    fill_grads(out, from_x, from_g, skip, hidden)


def fill_grads(out, from_x, from_g, skip, hidden):
    height = out.shape[0]
    for i in range(2):
        col = 3 * i * hidden
        out[:, col : col + 2 * hidden] = from_x[
            skip : skip + height, 2 * i * hidden : 2 * (i + 1) * hidden
        ]
        out[:, col + 2 * hidden : col + 3 * hidden] = from_g[
            skip : skip + height, i * hidden : (i + 1) * hidden
        ]


def each_half(part, height, body):
    reach = -(-height // 128) * 128

    @pl.when(part == 0)
    def _():
        body(0, 0)

    @pl.when(part == 1)
    def _():
        body(2 * height - reach, reach - height)


def forward_kernel(
    scalars, rows, weights, back, dab, hid, swap, rows_v, w_v, back_v, acts_v, total, sems
):
    n_z, both, _ = rows_v.shape
    chunk = w_v.shape[1]
    tok = both // 2
    hidden = hid.shape[1] // 2
    width = CHUNKS * chunk
    blocks, reach = swap.shape[0] - 1, swap.shape[-1]
    step = width // blocks

    def columns(k):
        return pl.ds(pl.multiple_of(k * chunk, 128), chunk)

    def row_copy(k):
        at = columns(k)
        return pltpu.make_async_copy(rows.at[:, :, at], rows_v.at[:, :, at], sems.at[0, k])

    def weight_copy(k):
        return pltpu.make_async_copy(weights.at[columns(k), :], w_v.at[k], sems.at[1, k])

    def back_copy(k):
        return pltpu.make_async_copy(back_v.at[k], back.at[:, columns(k)], sems.at[2, k])

    def swap_copy(n):
        at = pl.ds(pl.multiple_of(n * step + scalars[2] * (step - reach), 128), reach)
        return pltpu.make_async_copy(rows_v.at[:, :, at], swap.at[n], sems.at[3, n])

    acts_copy = pltpu.make_async_copy(acts_v, swap.at[blocks], sems.at[3, blocks])
    last = pl.ds(width, PAD)
    route_copy = pltpu.make_async_copy(rows.at[:, :, last], rows_v.at[:, :, last], sems.at[4, 0])

    for k in range(CHUNKS):
        weight_copy(k).start()
        row_copy(k).start()
    route_copy.start()

    for k in range(CHUNKS):
        row_copy(k).wait()
        weight_copy(k).wait()
        at = slice(k * chunk, (k + 1) * chunk)
        x_rows, g_rows = flat(rows_v[:, :tok, at]), flat(rows_v[:, tok:, at])
        from_x = jnp.dot(x_rows, w_v[k, :, : 4 * hidden], preferred_element_type=jnp.float32)
        from_g = jnp.dot(g_rows, w_v[k, :, 4 * hidden :], preferred_element_type=jnp.float32)
        if k == 0:
            total[:, : 4 * hidden] = from_x
            total[:, 4 * hidden :] = from_g
        else:
            total[:, : 4 * hidden] += from_x
            total[:, 4 * hidden :] += from_g
    route_copy.wait()
    for n in range(blocks):
        swap_copy(n).start()

    live_rows = flat(rows_v[:, :tok, width:]).astype(jnp.float32)
    gate_rows = flat(rows_v[:, tok:, width:]).astype(jnp.float32)
    lanes = lax.broadcasted_iota(jnp.int32, live_rows.shape, 1)
    for i in range(2):
        mine = lanes == scalars[i]
        live = jnp.sum(jnp.where(mine, live_rows, 0.0), axis=1, keepdims=True) > 0
        gate = jnp.sum(jnp.where(mine, gate_rows, 0.0), axis=1, keepdims=True)
        at = 2 * i * hidden
        act_a = total[:, at : at + hidden]
        act_b = total[:, at + hidden : at + 2 * hidden]
        grad_h = total[:, (4 + i) * hidden : (5 + i) * hidden] * gate
        sig = 1.0 / (1.0 + jnp.exp(-act_a))
        silu = act_a * sig
        grad_a = grad_h * act_b * sig * (1.0 + act_a * (1.0 - sig))
        dab[:, at : at + hidden] = jnp.where(live, grad_a, 0.0).astype(dab.dtype)
        dab[:, at + hidden : at + 2 * hidden] = jnp.where(live, grad_h * silu, 0.0).astype(dab.dtype)
        hid[:, i * hidden : (i + 1) * hidden] = jnp.where(live, silu * act_b * gate, 0.0).astype(
            hid.dtype
        )

    edge = 3 * hidden
    acts = jnp.concatenate(
        [dab[:, :edge], jnp.concatenate([dab[:, edge:], hid[...]], axis=1)], axis=0
    )
    acts_v[...] = acts.reshape(acts_v.shape)
    acts_copy.start()

    for k in range(CHUNKS):
        back_v[k] = lax.dot_general(
            dab[...],
            w_v[k, :, : 4 * hidden],
            (((1,), (1,)), ((), ())),
            preferred_element_type=jnp.float32,
        ).astype(back_v.dtype)
        back_copy(k).start()

    for k in range(CHUNKS):
        back_copy(k).wait()
    for n in range(blocks):
        swap_copy(n).wait()
    acts_copy.wait()


def forward(scalars, rows, weights):
    n_z, both, padded = rows.shape
    width, cols = weights.shape
    hidden, chunk, count = cols // 6, width // CHUNKS, n_z * both // 2
    reach = -(-width // (2 * BLOCKS) // 128) * 128
    bf16 = jnp.bfloat16
    vmem = pl.BlockSpec(memory_space=pltpu.VMEM)
    hbm = pl.BlockSpec(memory_space=pl.ANY)
    return pl.pallas_call(
        forward_kernel,
        out_shape=(
            jax.ShapeDtypeStruct((count, width), bf16),
            jax.ShapeDtypeStruct((count, 4 * hidden), bf16),
            jax.ShapeDtypeStruct((count, 2 * hidden), bf16),
            jax.ShapeDtypeStruct((BLOCKS + 1, n_z, both, reach), bf16),
        ),
        in_specs=[pl.BlockSpec(memory_space=pltpu.SMEM), hbm, hbm],
        out_specs=(hbm, vmem, vmem, hbm),
        scratch_shapes=[
            pltpu.VMEM((n_z, both, padded), bf16),
            pltpu.VMEM((CHUNKS, chunk, cols), bf16),
            pltpu.VMEM((CHUNKS, count, chunk), bf16),
            pltpu.VMEM((n_z, both, reach), bf16),
            pltpu.VMEM((count, cols), jnp.float32),
            pltpu.SemaphoreType.DMA((5, CHUNKS + BLOCKS)),
        ],
        compiler_params=pltpu.CompilerParams(vmem_limit_bytes=VMEM_LIMIT),
        cost_estimate=pl.CostEstimate(
            flops=2 * count * width * 10 * hidden, bytes_accessed=20_000_000, transcendentals=0
        ),
    )(scalars, rows, weights)


def grads_kernel(part, rows, dab, hid, out):
    count, height, _ = out.shape

    def half(start, skip):
        for n in range(count):
            put_grads(out.at[n], rows, 2 * height * n + start, skip, dab, hid)

    each_half(part[0], height, half)


def weight_grads(part, rows, dab, hid, per_step=2):
    n_z, both, padded = rows.shape
    height = (padded - PAD) // (2 * BLOCKS)
    count, cols = dab.shape[0], dab.shape[1] + hid.shape[1]
    return pl.pallas_call(
        grads_kernel,
        grid_spec=pltpu.PrefetchScalarGridSpec(
            num_scalar_prefetch=1,
            grid=(BLOCKS // per_step,),
            in_specs=[
                pl.BlockSpec((n_z, both, 2 * height * per_step), lambda i, part: (0, 0, i)),
                pl.BlockSpec(dab.shape, lambda i, part: (0, 0)),
                pl.BlockSpec(hid.shape, lambda i, part: (0, 0)),
            ],
            out_specs=pl.BlockSpec((per_step, height, cols), lambda i, part: (i, 0, 0)),
        ),
        out_shape=jax.ShapeDtypeStruct((BLOCKS, height, cols), jnp.bfloat16),
        compiler_params=pltpu.CompilerParams(vmem_limit_bytes=VMEM_SMALL),
        cost_estimate=pl.CostEstimate(
            flops=count * (padded - PAD) * cols, bytes_accessed=9_000_000, transcendentals=0
        ),
    )(jnp.reshape(part, (1,)).astype(jnp.int32), rows, dab, hid)


def other_kernel(place, keep_a, keep_b, got_a, got_b, acts, out_a, out_b, dab, hid):
    tok, hidden = got_a.shape[2] // 2, hid.shape[1] // 2
    count, cut, reach = dab.shape[0], keep_a.shape[1], got_a.shape[3]
    edge = 3 * hidden
    step = pl.program_id(0)

    @pl.when(step == 0)
    def _():
        rows = flat(acts[0])
        dab[:, :edge] = rows[:count]
        dab[:, edge:] = rows[count:, :hidden]
        hid[...] = rows[count:, hidden:]

    def dots(block, at, slices):
        columns = slice(at, at + 2 * hidden)
        pairs = pl.ds(pl.multiple_of(slices[0] * 2 * hidden, 128), slices[1] * 2 * hidden)
        ones = pl.ds(pl.multiple_of(slices[0] * hidden, 128), slices[1] * hidden)
        return dot_f32(block[:, :tok, columns], dab[:, pairs]), dot_f32(
            block[:, tok:, columns], hid[:, ones]
        )

    def put(start):
        from_x, from_g = dots(got_a[0], 0, (0, 2))
        rows = slice(start, start + cut)
        for i in range(2):
            col = 3 * i * hidden
            for at, part in (
                (col, from_x[rows, 2 * i * hidden : 2 * (i + 1) * hidden]),
                (col + 2 * hidden, from_g[rows, i * hidden : (i + 1) * hidden]),
            ):
                to = slice(at, at + part.shape[1])
                out_a[0, 0, :, to] = (keep_a[0, :, to].astype(jnp.float32) + part).astype(out_a.dtype)
        first = reach - 2 * hidden
        rows = slice(start + cut - first, start + 2 * cut - first)
        for m in range(2):
            from_x, from_g = dots(got_b[m], first, (place[8 + step], 1))
            for at, part in ((0, from_x[rows]), (2 * hidden, from_g[rows])):
                to = slice(at, at + part.shape[1])
                out_b[0, m, :, to] = (keep_b[m, :, to].astype(jnp.float32) + part).astype(out_b.dtype)

    @pl.when(place[12] == 0)
    def _():
        put(0)

    @pl.when(place[12] == 1)
    def _():
        put(reach - 2 * cut)


def core_sum(keep, got, slots):
    x, core, yh = lax.axis_index("x"), lax.axis_index("core"), lax.axis_index("yh")
    blocks, part, cols = keep.shape
    n_x, half, cut, width = blocks // 2, cols // 2, part // 2, blocks * part
    up = (x + core) % 2 == 0
    after, before = (x + 1) % 4, (x + 3) % 4
    a_slots = [x, jnp.where(up, after, before), jnp.where(up, before, after), (x + 2) % 4]
    far = jnp.where(core == 0, 1 - yh, yh)
    b_slots = [(yh, 0), (1 - far, 1), (far, 1), (1 - yh, 0)]
    place = [h * n_x + a_slots[s] for s in slots for h in range(2)]
    place += [h * 2 + m for h, _ in [b_slots[s] for s in slots] for m in range(2)]
    place += [c for _, c in [b_slots[s] for s in slots] for m in range(2)] + [core]
    place = jnp.stack([jnp.asarray(v, jnp.int32) for v in place])

    in_a = pl.BlockSpec((1, cut, cols), lambda j, p: (p[j], 0, 0))
    in_b = pl.BlockSpec((2, cut, half), lambda j, p: (p[4 + j], 1, p[8 + j]))

    def out(j, p):
        return (j // 2, j % 2, 0, 0)

    _, n_z, both, reach = got.shape
    count, hidden = n_z * both // 2, cols // 6
    return pl.pallas_call(
        other_kernel,
        grid_spec=pltpu.PrefetchScalarGridSpec(
            num_scalar_prefetch=1,
            grid=(4,),
            in_specs=[
                in_a,
                in_b,
                pl.BlockSpec((1, n_z, both, reach), lambda j, p: (p[j], 0, 0, 0)),
                pl.BlockSpec((2, n_z, both, reach), lambda j, p: (p[4 + j], 0, 0, 0)),
                pl.BlockSpec((1, n_z, both, reach), lambda j, p: (blocks, 0, 0, 0)),
            ],
            out_specs=[
                pl.BlockSpec((1, 1, cut, cols), out),
                pl.BlockSpec((1, 2, cut, half), out),
            ],
            scratch_shapes=[
                pltpu.VMEM((count, 4 * hidden), keep.dtype),
                pltpu.VMEM((count, 2 * hidden), keep.dtype),
            ],
        ),
        out_shape=[
            jax.ShapeDtypeStruct((2, 2, cut, cols), keep.dtype),
            jax.ShapeDtypeStruct((2, n_x, cut, half), keep.dtype),
        ],
        compiler_params=pltpu.CompilerParams(vmem_limit_bytes=VMEM_SMALL),
        cost_estimate=pl.CostEstimate(
            flops=count * width * cols, bytes_accessed=9_000_000, transcendentals=0
        ),
    )(place, keep, keep, got, got, got)


def pack_kernel(expert_index, slot, gate, tokens, out_grad, out):
    tok, width = tokens.shape
    out[:tok, :width] = tokens[...]
    out[tok:, :width] = out_grad[...]
    square = (tok, tok)
    eye = lax.broadcasted_iota(jnp.int32, square, 0) == lax.broadcasted_iota(jnp.int32, square, 1)

    def column(row):
        spread = jnp.broadcast_to(row.astype(jnp.float32), square)
        return jnp.sum(jnp.where(eye, spread, 0.0), axis=1, keepdims=True)

    lanes = lax.broadcasted_iota(jnp.int32, (tok, PAD), 1).astype(jnp.float32)
    live, weight = jnp.zeros((tok, PAD), jnp.float32), jnp.zeros((tok, PAD), jnp.float32)
    gates = gate[...].astype(jnp.float32)
    for r in range(expert_index.shape[0]):
        row = slice(r, r + 1)
        hit = (lanes == column(expert_index[row])) & (column(slot[row]) >= 0)
        live += jnp.where(hit, 1.0, 0.0)
        weight += jnp.where(hit, column(gates[row]), 0.0)
    out[:tok, width:] = live.astype(out.dtype)
    out[tok:, width:] = weight.astype(out.dtype)


def pack(tokens, out_grad, expert_index, slot, gate):
    tok, width = tokens.shape
    vmem = pl.BlockSpec(memory_space=pltpu.VMEM)
    return pl.pallas_call(
        pack_kernel,
        out_shape=jax.ShapeDtypeStruct((2 * tok, width + PAD), tokens.dtype),
        in_specs=[vmem] * 5,
        out_specs=vmem,
        compiler_params=pltpu.CompilerParams(vmem_limit_bytes=VMEM_LIMIT),
        cost_estimate=pl.CostEstimate(flops=0, bytes_accessed=700_000, transcendentals=0),
    )(expert_index.T, slot.T, gate.T, tokens, out_grad)


def add(*terms):
    return sum(t.astype(jnp.float32) for t in terms).astype(jnp.bfloat16)


def take(array, index, axis):
    return lax.dynamic_index_in_dim(array, index, axis, keepdims=False)


def pair_steps(place):
    return [
        [
            (place(p, c), place(p ^ 1 if (c + step) % 2 == 0 else 3 - p, c))
            for p in range(4)
            for c in range(2)
        ]
        for step in range(2)
    ]


X_RING = ("x", "core"), pair_steps(lambda p, c: p * 2 + c)
Y_RING = ("yh", "core", "yl"), pair_steps(lambda p, c: (p // 2 * 2 + c) * 2 + p % 2)


def pair_sum(ring, own, second, send):
    axes, (step1, step2) = ring
    got = lax.ppermute(send, axes, step1)
    last = lax.ppermute(add(second, got[1]), axes, step2)
    return add(own, got[0], last)


def x_blocks(blocks, axis):
    x, core = lax.axis_index("x"), lax.axis_index("core")
    up = (x + core) % 2 == 0
    after, before = (x + 1) % 4, (x + 3) % 4
    first, second = jnp.where(up, after, before), jnp.where(up, before, after)
    own, first, second, across = [take(blocks, at, axis) for at in (x, first, second, (x + 2) % 4)]
    return own, second, jnp.stack([first, across])


def y_blocks(blocks):
    yh, even = lax.axis_index("yh"), lax.axis_index("core") == 0
    cols = blocks.shape[-1] // 2
    here, there = take(blocks, yh, 0), take(blocks, 1 - yh, 0)
    near, far = here[..., cols:], there[..., cols:]
    first, second = jnp.where(even, near, far), jnp.where(even, far, near)
    return here[..., :cols], second, jnp.stack([first, there[..., :cols]])


def reduce_weights(swap, rows, dab, hid):
    core = lax.axis_index("core")
    got = lax.ppermute(swap, "core", SWAP)
    keep = weight_grads(core, rows, dab, hid)
    send_a, send_b = core_sum(keep, got, (1, 3))
    own_a, own_b = core_sum(keep, got, (0, 2))
    upper = pair_sum(X_RING, own_a[0], own_a[1], send_a)
    lower = pair_sum(Y_RING, own_b[0], own_b[1], send_b)
    upper = pair_sum(Y_RING, *y_blocks(upper))
    lower = pair_sum(X_RING, *x_blocks(lower, 0))
    return jnp.concatenate([upper, lower], axis=0)


def partner_weights(weights):
    core = lax.axis_index("core")
    half = take(weights.reshape(2, -1, weights.shape[1]), core, 0)
    mine = lax.ppermute(half, "yl", SWAP)
    other = lax.ppermute(mine, "core", SWAP)
    first = core == 0
    return jnp.concatenate([jnp.where(first, mine, other), jnp.where(first, other, mine)], axis=0)


def local(tokens, out_grad, expert_index, slot, gate, w_gate, w_up, w_down):
    tok, width = tokens.shape
    n_yl, n_z = lax.axis_size("yl"), lax.axis_size("z")
    hidden = w_gate.shape[2]
    yl, z = lax.axis_index("yl"), lax.axis_index("z")
    experts = [(row * n_z + z) // SPLIT for row in (yl, 1 - yl)]

    send = pack(tokens, out_grad, expert_index, slot, gate)
    rows = lax.all_gather(send, "z", axis=0, tiled=True)

    own = jnp.concatenate([w_gate[0], w_up[0], w_down[0]], axis=1)
    partner = partner_weights(own)
    pairs = 2 * hidden
    weights = jnp.concatenate(
        [own[:, :pairs], partner[:, :pairs], own[:, pairs:], partner[:, pairs:]], axis=1
    )

    rows = rows.reshape(n_z, 2 * tok, width + PAD)
    scalars = jnp.stack([*experts, 1 - lax.axis_index("core")]).astype(jnp.int32)
    back, dab, hid, swap = forward(scalars, rows, weights)
    grads = reduce_weights(swap, rows, dab, hid)
    input_grad = lax.psum_scatter(back, "z", scatter_dimension=0, tiled=True)
    return (
        input_grad,
        grads[None, :, :hidden],
        grads[None, :, hidden : 2 * hidden],
        grads[None, :, 2 * hidden :],
    )


def solution(mesh):
    fine = Mesh(mesh.devices.reshape(2, 4, 2, 2, 16), ("yh", "x", "core", "yl", "z"))
    every = P(("yh", "x", "core", "yl", "z"), None)
    slices = P(("yl", "z"), None, None)
    grads = P(("yl", "z"), ("yh", "x", "core"), None)
    return jax.shard_map(
        local,
        mesh=fine,
        in_specs=(every, every, every, every, every, slices, slices, slices),
        out_specs=(every, grads, grads, grads),
        check_vma=False,
    )
```
